256 devices in a mesh: frames: 64 (over z_hi, y, x), gz: 4 (over z_lo, core).
Axes of the slice: x: 4, y: 4, z: 8 (z_hi: 4, z_lo: 2; z = z_hi * 2 + z_lo), core: 2. Of those that a mesh axis runs over, the one named last changes fastest.
Arguments:
- recording: bfloat16 [128, 32, 1024, 128], P('frames', 'gz'), may hold values from -6 to 6
- group_ids: int32 [128], replicated, may hold values from 0 to 15, never falling along the last dimension, each value on 1 to 16 neighbouring positions
- shifts: float32 [16, 2], replicated, may hold values from -0.9 to 0.9
- fir_taps: float32 [31], replicated, may hold values from 0.05 to 1
Outputs:
- correlation: float32 [32, 1024, 128], P('gz', 'frames')
The draws below stay inside these ranges and needn't reach their ends.
Inputs may be any that keep to these rules, and one draw needn't show every extreme that they name: `group_ids`: frames of one group are consecutive: ids never fall along the frames, and every id occurs.
All inputs are finite; a program needn't handle non-finite values.
Results may differ from the reference program's by a relative error of at most 0.0033.
Values may be sent and summed in bfloat16 or wider, within the bound.
No kernel may reach another device: no remote copies, remote signals or barrier semaphores. Data moves between devices by JAX's collectives and lax.ppermute only.
A program may use at most 128 MiB of HBM per device.

```python
import math
import jax
import jax.numpy as jnp
import numpy as np
from jax import lax

F = 128
Z = 32
Y = 1024
X = 128
GROUPS = 16
TAPS = 31
RADIUS = 3


def steps_of(own_key, extent, split, least, largest):
    factor_of, own = 1.0, jax.random.fold_in(own_key, 6)
    for position, shards_of in split:
        heights = jnp.exp(jax.random.uniform(jax.random.fold_in(own, position), (shards_of,), jnp.float32, least / len(split), largest / len(split)))
        factor_of = factor_of * jnp.repeat(heights, extent[position] // shards_of).reshape([-1 if axis == position else 1 for axis in range(len(extent))])
    return factor_of


def split_up(count, total, limit, slope):
    portions = [(1 << 20) // math.isqrt(standing ** slope) + 1 for standing in range(2, count + 1)]
    rest, counts = total - limit - (count - 1), [1] * (count - 1)
    while rest > 0:
        free = [i for i in range(count - 1) if counts[i] < limit]
        mass, left = sum([portions[i] for i in free]), rest
        for i in free:
            addition = min(limit - counts[i], max(1, left * portions[i] // mass), rest)
            counts[i] = counts[i] + addition
            rest = rest - addition
    return np.array([limit] + counts)


def uneven_parts(rng, count, total, most, skew):
    if count == 2:
        one = jax.random.randint(rng, (), max(1, total - most), min(most, total - 1) + 1)
        return jnp.stack([one, total - one])
    lengths = jnp.asarray(split_up(count, total, most, skew), jnp.int32)
    couples = (count - 1) // 2
    source_of, sink = lengths[1:1 + 2 * couples:2], lengths[2:2 + 2 * couples:2]
    slack = jnp.minimum(source_of - 1, most - sink)
    passed = jax.random.randint(jax.random.fold_in(rng, 1), (couples,), 0, 1 << 20) % (slack + 1)
    lengths = lengths.at[1:1 + 2 * couples:2].set(source_of - passed).at[2:2 + 2 * couples:2].set(sink + passed)
    return lengths[jax.random.permutation(jax.random.fold_in(rng, 2), count)]


def scatter_about(own_key, shape, scale, bound, split=(), held_as=jnp.bfloat16):
    entries = jax.random.normal(own_key, shape, jnp.float32) * scale
    if len(split) > 0:
        entries = steps_of(own_key, shape, split, -0.22, 0.18) * entries
    return jnp.clip(entries, min=-bound, max=bound).astype(held_as)


def setup_inputs(seed: int = 0) -> dict:
    arg_keys = jax.random.split(jax.random.key(seed), 5)
    recording = scatter_about(arg_keys[0], (F, Z, Y, X), 1.0, 6.0, ((0, 64), (1, 4)))
    group_ids = jnp.searchsorted(jnp.cumsum(uneven_parts(arg_keys[1], GROUPS, F, 2 * F // GROUPS, 1)), jnp.arange(F), side="right").astype(jnp.int32)
    shifts = jnp.clip(jax.random.uniform(arg_keys[2], (GROUPS, 2), jnp.float32, -0.9, 0.9), -0.9, 0.9)
    fir_taps = jnp.clip(jnp.exp(jax.random.uniform(arg_keys[3], (TAPS,), jnp.float32, math.log(0.05), math.log(1.0))), 0.05, 1.0)
    return dict(recording=recording, group_ids=group_ids, shifts=shifts, fir_taps=fir_taps)


EPSILON = 1e-05
SIGMA_XY = 1.5
SIGMA_Z = 1.0

def gaussian(spread_sigma):
    offsets = jnp.arange(-RADIUS, RADIUS + 1).astype(jnp.float32)
    values = jnp.exp(-offsets * offsets / (2.0 * spread_sigma * spread_sigma))
    return values / jnp.sum(values)

def band_matrix(weights, length):
    reach = (weights.shape[0] - 1) // 2
    cells = jnp.arange(length).astype(jnp.int32)
    offsets = jnp.arange(-reach, reach + 1).astype(jnp.int32)
    distance = cells[:, None] - cells[None, :]
    hits = (distance[:, :, None] == offsets[None, None, :]).astype(jnp.float32)
    return lax.optimization_barrier(jnp.sum(hits * weights[None, None, :], axis=-1))

def fir_matrix(fir_taps, length):
    matrix = jnp.transpose(band_matrix(fir_taps, length))
    return (matrix / lax.optimization_barrier(jnp.sum(matrix, axis=1, keepdims=True))).astype(jnp.bfloat16)

def frame_shifts(local_groups, shifts):
    groups = jnp.arange(shifts.shape[0]).astype(jnp.int32)
    onehot = (local_groups[:, None] == groups[None, :]).astype(jnp.float32)
    per_frame = jnp.dot(onehot, shifts, precision=lax.Precision.HIGHEST)
    return (per_frame[:, 0], per_frame[:, 1])

def shift_weights(shift_value):
    shaped = shift_value[:, None, None, None]
    return (jnp.maximum(shaped, 0.0), 1.0 - jnp.abs(shaped), jnp.maximum(-shaped, 0.0))

def register_frames(extended, shift_y, shift_x):
    values = extended.astype(jnp.float32)
    weight_back, weight_here, weight_ahead = shift_weights(shift_x)
    padded = jnp.pad(values, ((0, 0), (0, 0), (0, 0), (1, 1)))
    values = weight_back * padded[..., :-2] + weight_here * padded[..., 1:-1] + weight_ahead * padded[..., 2:]
    weight_back, weight_here, weight_ahead = shift_weights(shift_y)
    return weight_back * values[:, :, :-2] + weight_here * values[:, :, 1:-1] + weight_ahead * values[:, :, 2:]

def filter_block(registered, filter_rows):
    shape = registered.shape
    columns = registered.reshape(shape[0], -1)
    baseline = jnp.dot(filter_rows, columns, preferred_element_type=jnp.float32)
    detrended = columns.astype(jnp.float32) - baseline
    average = lax.optimization_barrier(jnp.mean(detrended, axis=0, keepdims=True))
    centred = detrended - average
    spread = jnp.sqrt(lax.optimization_barrier(jnp.mean(centred * centred, axis=0, keepdims=True)) + EPSILON)
    return (centred / spread).astype(jnp.bfloat16).reshape(shape)

def along_x(block, matrix):
    shape = block.shape
    rows = block.reshape(-1, shape[-1])
    return jnp.dot(rows, matrix, preferred_element_type=jnp.float32).astype(jnp.bfloat16).reshape(shape)

def reference(recording, group_ids, shifts, fir_taps):
    shift_y, shift_x = frame_shifts(group_ids, shifts)
    filter_rows = fir_matrix(fir_taps, F)

    def one_plane(plane_index):
        plane = lax.dynamic_index_in_dim(recording, plane_index, 1, keepdims=True)
        padded = jnp.pad(plane, ((0, 0), (0, 0), (1, 1), (0, 0)))
        registered = register_frames(padded, shift_y, shift_x).astype(jnp.bfloat16)
        return filter_block(registered, filter_rows)[:, 0]
    normed = lax.map(one_plane, jnp.arange(Z).astype(jnp.int32))
    kernel_x = gaussian(SIGMA_XY).astype(jnp.bfloat16)
    kernel_y = gaussian(SIGMA_XY)
    kernel_z = gaussian(SIGMA_Z)
    matrix_x = band_matrix(kernel_x.astype(jnp.float32), X).astype(jnp.bfloat16)
    center = kernel_z[RADIUS] * kernel_y[RADIUS] * kernel_x[RADIUS].astype(jnp.float32)

    def one_frame(frame_index, running):
        frame = lax.dynamic_index_in_dim(normed, frame_index, 1, keepdims=False)
        smooth_x = along_x(frame, matrix_x).astype(jnp.float32)
        padded = jnp.pad(smooth_x, ((RADIUS, RADIUS), (RADIUS, RADIUS), (0, 0)))
        rows_y = padded.shape[1] - 2 * RADIUS
        planes = padded.shape[0] - 2 * RADIUS
        partial_value = jnp.zeros((padded.shape[0], rows_y, X), jnp.float32)
        for step in range(2 * RADIUS + 1):
            partial_value = partial_value + kernel_y[step] * padded[:, step:step + rows_y]
        smoothed = jnp.zeros((planes, rows_y, X), jnp.float32)
        for step in range(2 * RADIUS + 1):
            smoothed = smoothed + kernel_z[step] * partial_value[step:step + planes]
        values = frame.astype(jnp.float32)
        return running + values * (smoothed - center * values)
    running = lax.fori_loop(0, F, one_frame, jnp.zeros((Z, Y, X), jnp.float32))
    return running / (F * (1.0 - center))
```

```python
import functools

import jax
import jax.numpy as jnp
import numpy as np
from jax import lax
from jax.experimental import pallas as pl
from jax.experimental.pallas import tpu as pltpu
from jax.sharding import PartitionSpec as P

RADIUS = 3
EPSILON = 1e-05
SIGMA_XY = 1.5
SIGMA_Z = 1.0
VMEM = 56 * 1024 * 1024


def gaussian(sigma):
    offsets = np.arange(-RADIUS, RADIUS + 1).astype(np.float32)
    values = np.exp(-offsets * offsets / np.float32(2.0 * sigma * sigma)).astype(np.float32)
    return (values / values.sum(dtype=np.float32)).astype(np.float32)


KERNEL_X = gaussian(SIGMA_XY).astype(jnp.bfloat16).astype(np.float32)
KERNEL_Y = gaussian(SIGMA_XY)
KERNEL_Z = gaussian(SIGMA_Z)
CENTER = float(np.float32(np.float32(KERNEL_Z[RADIUS] * KERNEL_Y[RADIUS]) * KERNEL_X[RADIUS]))


def params(*semantics):
    return pltpu.CompilerParams(dimension_semantics=semantics, vmem_limit_bytes=VMEM)


def register_kernel(first_ref, groups_ref, shifts_ref, x_ref, out_ref, aligned):
    frame = pl.program_id(0)
    rows, width = x_ref.shape[2], x_ref.shape[3]
    tile = out_ref.shape[3]
    group = groups_ref[first_ref[0] + frame]
    shift_y, shift_x = shifts_ref[group, 0], shifts_ref[group, 1]
    lane = lax.broadcasted_iota(jnp.int32, (8, width), 1)
    back = shift_x > 0.0
    edge = jnp.where(back, 0, width - 1)
    roll = jnp.where(back, 1, width - 1)
    side_x = jnp.where(lane == edge, 0.0, jnp.abs(shift_x))[None]
    here_x = 1.0 - jnp.abs(shift_x)
    zeros = jnp.zeros((8, width), jnp.float32)
    aligned[0:8] = zeros
    aligned[rows + 8 : rows + 16] = zeros
    step = min(128, rows)
    for start in range(0, rows, step):
        values = x_ref[0, 0, start : start + step].astype(jnp.float32)
        moved = pltpu.roll(values, roll, 1).reshape(step // 8, 8, width)
        mixed = here_x * values.reshape(step // 8, 8, width) + side_x * moved
        aligned[8 + start : 8 + start + step] = mixed.reshape(step, width)
    here_y, side_y = 1.0 - jnp.abs(shift_y), jnp.abs(shift_y)

    def finish(offset):
        for start in range(0, rows, step):
            here = aligned[8 + start : 8 + start + step]
            beside = aligned[8 + offset + start : 8 + offset + start + step]
            mixed = (here_y * here + side_y * beside).astype(out_ref.dtype)
            out_ref[start // tile : (start + step) // tile, 0, 0] = mixed.reshape(step // tile, tile, width)

    pl.when(shift_y > 0.0)(lambda: finish(-1))
    pl.when(shift_y <= 0.0)(lambda: finish(1))


def register(recording, group_ids, shifts, first, planes, tiles):
    frames, _, rows, width = recording.shape
    tile = rows // tiles
    low, gap, after = planes
    count = low + after

    def plane(j):
        return jnp.where(j < low, j, j + gap) if low else j + gap

    smem = pl.BlockSpec(memory_space=pltpu.SMEM)
    return pl.pallas_call(
        register_kernel,
        grid=(frames, count),
        in_specs=[smem, smem, smem, pl.BlockSpec((1, 1, rows, width), lambda f, j: (f, plane(j), 0, 0))],
        out_specs=pl.BlockSpec((tiles, 1, 1, tile, width), lambda f, j: (0, f, j, 0, 0)),
        out_shape=jax.ShapeDtypeStruct((tiles, frames, count, tile, width), recording.dtype),
        scratch_shapes=[pltpu.VMEM((rows + 16, width), jnp.float32)],
        compiler_params=params("arbitrary", "arbitrary"),
        name="register",
    )(first, group_ids, shifts, recording)


def filter_kernel(taps_ref, x_ref, out_ref, matrix, rows):
    frames, tile, width = x_ref.shape[0], x_ref.shape[2], x_ref.shape[3]
    taps = taps_ref.shape[0]
    reach = (taps - 1) // 2

    @pl.when(pl.program_id(0) == 0)
    def _():
        t = lax.broadcasted_iota(jnp.int32, (frames, frames), 0)
        u = lax.broadcasted_iota(jnp.int32, (frames, frames), 1)
        distance = u - t + reach
        band = jnp.zeros((frames, frames), jnp.float32)
        for k in range(taps):
            band = jnp.where(distance == k, taps_ref[k], band)
        matrix[...] = (band / jnp.sum(band, axis=1, keepdims=True)).astype(matrix.dtype)

    rows[...] = x_ref[:, 0].astype(jnp.float32).reshape(frames * tile, width)
    weights = matrix[...]
    for y in range(tile):
        values = rows[pl.ds(y, frames, stride=tile), :]
        baseline = jnp.dot(weights, values.astype(jnp.bfloat16), preferred_element_type=jnp.float32)
        detrended = values - baseline
        average = jnp.sum(detrended, axis=0, keepdims=True) * (1.0 / frames)
        centred = detrended - average
        power = jnp.sum(centred * centred, axis=0, keepdims=True) * (1.0 / frames)
        out_ref[0, y] = (centred * lax.rsqrt(power + EPSILON)).astype(out_ref.dtype)


def filter_planes(registered, fir_taps):
    frames, planes, tile, width = registered.shape
    return pl.pallas_call(
        filter_kernel,
        grid=(planes,),
        in_specs=[
            pl.BlockSpec(memory_space=pltpu.SMEM),
            pl.BlockSpec((frames, 1, tile, width), lambda z: (0, z, 0, 0)),
        ],
        out_specs=pl.BlockSpec((1, tile, frames, width), lambda z: (z, 0, 0, 0)),
        out_shape=jax.ShapeDtypeStruct((planes, tile, frames, width), registered.dtype),
        scratch_shapes=[pltpu.VMEM((frames, frames), jnp.bfloat16), pltpu.VMEM((frames * tile, width), jnp.float32)],
        compiler_params=params("arbitrary"),
        name="filter",
    )(fir_taps, registered)


def pair_sums(parts, taps):
    total = taps[RADIUS] * parts[RADIUS]
    for k in range(RADIUS):
        total = total + taps[k] * (parts[k] + parts[2 * RADIUS - k])
    return total


def correlate_kernel(spots, *refs):
    pieces = refs[: len(spots)]
    centers = refs[len(spots) : -5]
    out_ref, current, ring, mixed, matrix = refs[-5:]
    planes, tile = out_ref.shape[0], out_ref.shape[1]
    frames, width = current.shape[1], current.shape[2]
    step = pl.program_id(0)
    row = step - RADIUS
    taps_y = [float(v) for v in KERNEL_Y]
    taps_z = [float(v) for v in KERNEL_Z]

    @pl.when(step == 0)
    def _():
        distance = lax.broadcasted_iota(jnp.int32, (width, width), 1) - lax.broadcasted_iota(
            jnp.int32, (width, width), 0
        )
        band = jnp.zeros((width, width), jnp.float32)
        for k in range(2 * RADIUS + 1):
            band = jnp.where(distance == k - RADIUS, float(KERNEL_X[k]), band)
        matrix[...] = band.astype(matrix.dtype)

    def fill(zone):
        for (where, first), piece in zip(spots, pieces):
            if where == zone:
                for source, target in first:
                    current[target] = piece[source, 0]

    pl.when(row < 0)(lambda: fill(0))
    pl.when((row >= 0) & (row < tile))(lambda: fill(1))
    pl.when(row >= tile)(lambda: fill(2))

    window = 2 * RADIUS + 1
    slot = lax.rem(step, window)
    for start in range(0, frames, 16):
        parts = [current[z, start : start + 16].astype(jnp.float32) for z in range(planes + 2 * RADIUS)]
        for z in range(planes):
            ring[slot, z, start : start + 16] = pair_sums(parts[z : z + window], taps_z)

    @pl.when(step >= 2 * RADIUS)
    def _():
        y = step - 2 * RADIUS
        slots = [lax.rem(step + 1 + k, window) for k in range(window)]
        plane_of = {}
        inner = [first for zone, first in spots if zone == 1 and RADIUS <= first[0][1] < RADIUS + planes]
        for first, piece in zip(inner, centers):
            for source, target in first:
                plane_of[target - RADIUS] = (piece, source)
        for z in range(planes):
            for start in range(0, frames, 32):
                parts = [ring[s, z, start : start + 32] for s in slots]
                mixed[z, start : start + 32] = pair_sums(parts, taps_y).astype(mixed.dtype)
        for z in range(planes):
            smoothed = jnp.dot(mixed[z], matrix[...], preferred_element_type=jnp.float32)
            piece, source = plane_of[z]
            values = piece[source, 0].astype(jnp.float32)
            total = jnp.sum(values * (smoothed - CENTER * values), axis=0, keepdims=True)
            out_ref[z, pl.ds(y, 1), :] = total * (1.0 / (frames * (1.0 - CENTER)))


def correlate(planes, tile, pieces):
    frames, width = pieces[0][2].shape[2:]

    def spec(zone, array, lag=0):
        count, rows = array.shape[:2]
        begin = (0, RADIUS, RADIUS + tile)[zone] + lag
        return pl.BlockSpec(
            (count, 1, frames, width), lambda i: (0, jnp.clip(i - begin, 0, rows - 1), 0, 0)
        )

    spots = [(zone, spot) for zone, spot, _ in pieces]
    inner = [p for p in pieces if p[0] == 1 and RADIUS <= p[1][0][1] < RADIUS + planes]
    arrays = [p[2] for p in pieces] + [p[2] for p in inner]
    specs = [spec(p[0], p[2]) for p in pieces] + [spec(1, p[2], RADIUS) for p in inner]
    return pl.pallas_call(
        functools.partial(correlate_kernel, spots),
        grid=(tile + 2 * RADIUS,),
        in_specs=specs,
        out_specs=pl.BlockSpec((planes, tile, width), lambda i: (0, 0, 0)),
        out_shape=jax.ShapeDtypeStruct((planes, tile, width), jnp.float32),
        scratch_shapes=[
            pltpu.VMEM((planes + 2 * RADIUS, frames, width), jnp.bfloat16),
            pltpu.VMEM((2 * RADIUS + 1, planes, frames, width), jnp.float32),
            pltpu.VMEM((planes, frames, width), jnp.bfloat16),
            pltpu.VMEM((width, width), jnp.bfloat16),
        ],
        compiler_params=params("arbitrary"),
        name="correlate",
    )(*arrays)


def body(recording, group_ids, shifts, fir_taps):
    planes, rows = recording.shape[1], recording.shape[2]
    tiles, slabs = lax.axis_size("frames"), lax.axis_size("gz")
    tile = rows // tiles
    first = (lax.axis_index("frames") * recording.shape[0]).reshape(1)
    both = ("frames", "gz")

    def send(array, up_y, up_z):
        pairs = [
            (t * slabs + g, (t + up_y) * slabs + g + up_z)
            for t in range(tiles)
            for g in range(slabs)
            if 0 <= t + up_y < tiles and 0 <= g + up_z < slabs
        ]
        return lax.ppermute(array, both, pairs)

    sent = register(recording, group_ids, shifts, first, (0, 0, planes), tiles)
    arrived = lax.all_to_all(sent, "frames", 0, 0)
    normed = filter_planes(arrived.reshape(-1, planes, tile, recording.shape[3]), fir_taps)
    spans = {0: (0, planes), 1: (planes - RADIUS, planes), -1: (0, RADIUS)}
    starts = {0: RADIUS, 1: 0, -1: RADIUS + planes}
    pieces = [(1, [(z, z + RADIUS) for z in range(planes)], normed)]
    for up_y in (1, -1, 0):
        for up_z in (0, 1, -1):
            if up_y or up_z:
                z0, z1 = spans[up_z]
                y0, y1 = {0: (0, tile), 1: (tile - RADIUS, tile), -1: (0, RADIUS)}[up_y]
                moved = send(normed[z0:z1, y0:y1], up_y, up_z)
                zone = {1: 0, 0: 1, -1: 2}[up_y]
                pieces.append((zone, [(z, z + starts[up_z]) for z in range(z1 - z0)], moved))
    return correlate(planes, tile, pieces)


def solution(mesh):
    placed = (P("frames", "gz", None, None), P(), P(), P())
    return jax.shard_map(
        body, mesh=mesh, in_specs=placed, out_specs=P("gz", "frames", None), check_vma=False
    )
```

```python
import functools

import jax
import jax.numpy as jnp
import numpy as np
from jax import lax
from jax.experimental import pallas as pl
from jax.experimental.pallas import tpu as pltpu
from jax.sharding import PartitionSpec as P

RADIUS = 3
EPSILON = 1e-05
SIGMA_XY = 1.5
SIGMA_Z = 1.0
HALF = 4
VMEM = 56 * 1024 * 1024


def gaussian(sigma):
    offsets = np.arange(-RADIUS, RADIUS + 1).astype(np.float32)
    values = np.exp(-offsets * offsets / np.float32(2.0 * sigma * sigma)).astype(np.float32)
    return (values / values.sum(dtype=np.float32)).astype(np.float32)


KERNEL_X = gaussian(SIGMA_XY).astype(jnp.bfloat16).astype(np.float32)
KERNEL_Y = gaussian(SIGMA_XY)
KERNEL_Z = gaussian(SIGMA_Z)
CENTER = float(np.float32(np.float32(KERNEL_Z[RADIUS] * KERNEL_Y[RADIUS]) * KERNEL_X[RADIUS]))


COST = pl.CostEstimate(flops=1, bytes_accessed=1, transcendentals=0)


def params(*semantics):
    return pltpu.CompilerParams(dimension_semantics=semantics, vmem_limit_bytes=VMEM)


def register_kernel(first_ref, groups_ref, shifts_ref, x_ref, out_ref, aligned):
    frame = pl.program_id(0)
    planes, rows, width = x_ref.shape[1:]
    tile = rows // out_ref.shape[0]
    group = groups_ref[first_ref[0] + frame]
    shift_y, shift_x = shifts_ref[group, 0], shifts_ref[group, 1]
    lane = lax.broadcasted_iota(jnp.int32, (8, width), 1)
    upper = lax.broadcasted_iota(jnp.int32, (8, width), 0) < HALF
    back = shift_x > 0.0
    edge = jnp.where(back, 0, width - 1)
    roll = jnp.where(back, 1, width - 1)
    side_x = jnp.where(lane == edge, 0.0, jnp.abs(shift_x))[None]
    here_x = 1.0 - jnp.abs(shift_x)
    zeros = jnp.zeros((8, width), jnp.float32)
    step = min(128, rows)
    for plane in range(planes):
        aligned[plane, 0:8] = zeros
        aligned[plane, rows + 8 : rows + 16] = zeros
        for start in range(0, rows, step):
            values = x_ref[0, plane, start : start + step].astype(jnp.float32)
            moved = pltpu.roll(values, roll, 1).reshape(step // 8, 8, width)
            mixed = here_x * values.reshape(step // 8, 8, width) + side_x * moved
            aligned[plane, 8 + start : 8 + start + step] = mixed.reshape(step, width)
    here_y, side_y = 1.0 - jnp.abs(shift_y), jnp.abs(shift_y)

    def finish(offset):
        def unit(plane, row):
            here = aligned[plane, 8 + row : 16 + row]
            beside = aligned[plane, 8 + offset + row : 16 + offset + row]
            return here_y * here + side_y * beside

        before = [unit(plane, -HALF) for plane in range(planes)]
        for t in range(rows // tile):
            middle, ends = [], []
            for plane in range(planes):
                middle.append(unit(plane, t * tile + HALF))
                after = unit(plane, t * tile + tile - HALF)
                ends.append(jnp.where(upper, after, before[plane]))
                before[plane] = after
            out_ref[t, 0, 0] = jnp.concatenate(ends, axis=0).astype(out_ref.dtype)
            out_ref[t, 0, 1] = jnp.concatenate(middle, axis=0).astype(out_ref.dtype)

    pl.when(shift_y > 0.0)(lambda: finish(-1))
    pl.when(shift_y <= 0.0)(lambda: finish(1))


def register(recording, group_ids, shifts, first, tiles):
    frames, planes, rows, width = recording.shape
    smem = pl.BlockSpec(memory_space=pltpu.SMEM)
    return pl.pallas_call(
        register_kernel,
        grid=(frames, planes // 2),
        in_specs=[smem, smem, smem, pl.BlockSpec((1, 2, rows, width), lambda f, j: (f, j, 0, 0))],
        out_specs=pl.BlockSpec((tiles, 1, 2, 16, width), lambda f, j: (0, f, 0, j, 0)),
        out_shape=jax.ShapeDtypeStruct((tiles, frames, 2, planes * 8, width), recording.dtype),
        scratch_shapes=[pltpu.VMEM((2, rows + 16, width), jnp.float32)],
        cost_estimate=COST,
        compiler_params=params("arbitrary", "arbitrary"),
        name="register",
    )(first, group_ids, shifts, recording)


def filter_kernel(part, taps_ref, x_ref, out_ref, low_ref, high_ref, *rest):
    matrix, rows = rest[-2:]
    frames, _, tile, width = x_ref.shape
    planes = out_ref.shape[0]
    taps = taps_ref.shape[0]
    reach = (taps - 1) // 2
    step = pl.program_id(0)

    @pl.when(step == 0)
    def _():
        t = lax.broadcasted_iota(jnp.int32, (frames, frames), 0)
        u = lax.broadcasted_iota(jnp.int32, (frames, frames), 1)
        distance = u - t + reach
        band = jnp.zeros((frames, frames), jnp.float32)
        for k in range(taps):
            band = jnp.where(distance == k, taps_ref[k], band)
        matrix[...] = (band / jnp.sum(band, axis=1, keepdims=True)).astype(matrix.dtype)

    rows[...] = x_ref[...].astype(jnp.float32).reshape(frames * tile, width)
    weights = matrix[...]
    for cell in range(tile):
        values = rows[pl.ds(cell, frames, stride=tile), :]
        baseline = jnp.dot(weights, values.astype(jnp.bfloat16), preferred_element_type=jnp.float32)
        detrended = values - baseline
        average = jnp.sum(detrended, axis=0, keepdims=True) * (1.0 / frames)
        centred = detrended - average
        power = jnp.sum(centred * centred, axis=0, keepdims=True) * (1.0 / frames)
        out_ref[cell // 8, cell % 8] = (centred * lax.rsqrt(power + EPSILON)).astype(out_ref.dtype)
    for p in range(planes):
        plane = step * planes + p

        @pl.when(plane < RADIUS)
        def _():
            low_ref[plane] = out_ref[p]

        first = pl.num_programs(0) * planes - RADIUS

        @pl.when(plane >= first)
        def _():
            high_ref[plane - first] = out_ref[p]

        if part == 0:
            rest[0][p] = out_ref[p, HALF - RADIUS : HALF]
            rest[1][p] = out_ref[p, HALF : HALF + RADIUS]


def filter_cells(registered, fir_taps, part):
    frames, _, cells, width = registered.shape
    planes = cells // 8

    def shape(*size):
        return jax.ShapeDtypeStruct((*size, frames, width), registered.dtype)

    slab = pl.BlockSpec((RADIUS, 8, frames, width), lambda z: (0, 0, 0, 0))
    rows = pl.BlockSpec((2, RADIUS, frames, width), lambda z: (z, 0, 0, 0))
    return pl.pallas_call(
        functools.partial(filter_kernel, part),
        grid=(planes // 2,),
        in_specs=[
            pl.BlockSpec(memory_space=pltpu.SMEM),
            pl.BlockSpec((frames, 1, 16, width), lambda z: (0, part, z, 0)),
        ],
        out_specs=[pl.BlockSpec((2, 8, frames, width), lambda z: (z, 0, 0, 0)), slab, slab] + [rows, rows][: 2 - 2 * part],
        out_shape=[shape(planes, 8), shape(RADIUS, 8), shape(RADIUS, 8)] + [shape(planes, RADIUS)] * (2 - 2 * part),
        scratch_shapes=[pltpu.VMEM((frames, frames), jnp.bfloat16), pltpu.VMEM((frames * 16, width), jnp.float32)],
        cost_estimate=COST,
        compiler_params=params("arbitrary"),
        name="filter",
    )(fir_taps, registered)


def pair_sums(parts, taps):
    total = taps[RADIUS] * parts[RADIUS]
    for k in range(RADIUS):
        total = total + taps[k] * (parts[k] + parts[2 * RADIUS - k])
    return total


TAPS_Y = [float(v) for v in KERNEL_Y]
TAPS_Z = [float(v) for v in KERNEL_Z]
WINDOW = 2 * RADIUS + 1
SCRATCH = 16


def smooth_z(current, target):
    planes = target.shape[0]
    for start in range(0, current.shape[1], 16):
        parts = [current[z, start : start + 16].astype(jnp.float32) for z in range(planes + 2 * RADIUS)]
        for z in range(planes):
            target[z, start : start + 16] = pair_sums(parts[z : z + WINDOW], TAPS_Z)


def band_of(matrix):
    width = matrix.shape[0]
    distance = lax.broadcasted_iota(jnp.int32, (width, width), 1) - lax.broadcasted_iota(
        jnp.int32, (width, width), 0
    )
    band = jnp.zeros((width, width), jnp.float32)
    for k in range(WINDOW):
        band = jnp.where(distance == k - RADIUS, float(KERNEL_X[k]), band)
    matrix[...] = band.astype(matrix.dtype)


def row_of_image(mixed, values_of, matrix, out_ref, y):
    for z in range(mixed.shape[0]):
        smoothed = jnp.dot(mixed[z], matrix[...], preferred_element_type=jnp.float32)
        values = values_of(z).astype(jnp.float32)
        frames = values.shape[0]
        total = jnp.sum(values * (smoothed - CENTER * values), axis=0, keepdims=True)
        out_ref[z, pl.ds(y, 1), :] = total * (1.0 / (frames * (1.0 - CENTER)))


def inner_kernel(ends, middle, low_ends, high_ends, low_middle, high_middle, out_ref, part_ref, *scratch):
    current, ring, mixed, values, matrix = scratch
    planes, tile = out_ref.shape[0], out_ref.shape[1]
    frames = current.shape[1]
    band_of(matrix)
    for row in range(RADIUS):
        ring[row] = jnp.zeros(ring.shape[1:], ring.dtype)

    def take(y):
        inside = (y >= HALF) & (y < tile - HALF)
        row = jnp.where(inside, y - HALF, jnp.where(y < HALF, y + HALF, y - (tile - HALF)))

        def fill(low, own, high):
            for k in range(RADIUS):
                current[k] = low[k, row]
                current[RADIUS + planes + k] = high[k, row]
            for z in range(planes):
                current[RADIUS + z] = own[z, row]

        pl.when(inside)(lambda: fill(low_middle, middle, high_middle))
        pl.when(jnp.logical_not(inside))(lambda: fill(low_ends, ends, high_ends))
        smooth_z(current, ring.at[lax.rem(y + RADIUS, WINDOW)])

    def rows_of(y, z, start):
        return pair_sums([ring[lax.rem(y + k, WINDOW), z, start : start + 32] for k in range(WINDOW)], TAPS_Y)

    def give_part(y, at):
        for z in range(planes):
            for start in range(0, frames, 32):
                part_ref[at, z, start : start + 32] = rows_of(y, z, start)

    def give(y):
        inside = (y >= HALF) & (y < tile - HALF)
        row = jnp.where(inside, y - HALF, jnp.where(y < HALF, y + HALF, y - (tile - HALF)))

        def fill(own):
            for z in range(planes):
                values[z] = own[z, row]

        pl.when(inside)(lambda: fill(middle))
        pl.when(jnp.logical_not(inside))(lambda: fill(ends))
        for z in range(planes):
            for start in range(0, frames, 32):
                mixed[z, start : start + 32] = rows_of(y, z, start).astype(mixed.dtype)
        row_of_image(mixed, lambda z: values[z], matrix, out_ref, y)

    pl.loop(0, RADIUS)(take)

    @pl.loop(RADIUS, 2 * RADIUS)
    def _(y):
        take(y)
        give_part(y - RADIUS, y - RADIUS)

    @pl.loop(2 * RADIUS, tile)
    def _(y):
        take(y)
        give(y - RADIUS)

    @pl.loop(tile, tile + RADIUS)
    def _(y):
        slot = lax.rem(y + RADIUS, WINDOW)
        ring[slot] = jnp.zeros(ring.shape[1:], ring.dtype)
        give_part(y - RADIUS, y - tile + RADIUS)


def outer_kernel(ends, part, image, *refs):
    sides, (out_ref, current, halo, mixed, matrix) = refs[:-5], refs[-5:]
    planes, tile = out_ref.shape[0], out_ref.shape[1]
    frames = current.shape[1]
    band_of(matrix)
    out_ref[...] = image[...]

    def side(low, own, high, first, upper):
        @pl.loop(0, RADIUS)
        def _(k):
            for j in range(RADIUS):
                current[j] = low[j, first + k]
                current[RADIUS + planes + j] = high[j, first + k]
            for z in range(planes):
                current[RADIUS + z] = own[z, k]
            smooth_z(current, halo.at[k])

        for n in range(RADIUS):
            y = tile - RADIUS + n if upper else n
            taps = [((tile + k if upper else k - RADIUS) - y + RADIUS, k) for k in range(RADIUS)]
            taps = [(TAPS_Y[at], k) for at, k in taps if 0 <= at < WINDOW]
            for z in range(planes):
                for start in range(0, frames, 32):
                    total = part[n + RADIUS * upper, z, start : start + 32]
                    for tap, k in taps:
                        total = total + tap * halo[k, z, start : start + 32]
                    mixed[z, start : start + 32] = total.astype(mixed.dtype)
            row = y - (tile - HALF) if upper else y + HALF
            row_of_image(mixed, lambda z: ends[z, row], matrix, out_ref, y)

    below, above, low_corners, high_corners = sides
    side(low_corners, below, high_corners, 0, 0)
    side(low_corners, above, high_corners, RADIUS, 1)


def inner(ends, middle, slabs_ends, slabs_middle, tile):
    planes, _, frames, width = ends.shape
    vmem = pl.BlockSpec(memory_space=pltpu.VMEM)
    return pl.pallas_call(
        inner_kernel,
        in_specs=[vmem] * 6,
        out_specs=[vmem] * 2,
        out_shape=[
            jax.ShapeDtypeStruct((planes, tile, width), jnp.float32),
            jax.ShapeDtypeStruct((2 * RADIUS, planes, frames, width), jnp.float32),
        ],
        scratch_shapes=[
            pltpu.VMEM((planes + 2 * RADIUS, frames, width), jnp.bfloat16),
            pltpu.VMEM((WINDOW, planes, frames, width), jnp.float32),
            pltpu.VMEM((planes, frames, width), jnp.bfloat16),
            pltpu.VMEM((planes, frames, width), jnp.bfloat16),
            pltpu.VMEM((width, width), jnp.bfloat16),
        ],
        cost_estimate=COST,
        compiler_params=pltpu.CompilerParams(vmem_limit_bytes=SCRATCH * 2**21),
        name="inner",
    )(ends, middle, *slabs_ends, *slabs_middle)


def outer(ends, part, image, below, above, corners):
    planes, _, frames, width = ends.shape
    vmem = pl.BlockSpec(memory_space=pltpu.VMEM)
    return pl.pallas_call(
        outer_kernel,
        in_specs=[vmem] * 7,
        out_specs=vmem,
        out_shape=jax.ShapeDtypeStruct(image.shape, jnp.float32),
        scratch_shapes=[
            pltpu.VMEM((planes + 2 * RADIUS, frames, width), jnp.bfloat16),
            pltpu.VMEM((RADIUS, planes, frames, width), jnp.float32),
            pltpu.VMEM((planes, frames, width), jnp.bfloat16),
            pltpu.VMEM((width, width), jnp.bfloat16),
        ],
        cost_estimate=COST,
        compiler_params=pltpu.CompilerParams(vmem_limit_bytes=SCRATCH * 2**21),
        name="outer",
    )(ends, part, image, below, above, *corners)


def body(recording, group_ids, shifts, fir_taps):
    planes, rows = recording.shape[1], recording.shape[2]
    tiles, slabs = lax.axis_size("frames"), lax.axis_size("gz")
    tile = rows // tiles
    first = (lax.axis_index("frames") * recording.shape[0]).reshape(1)

    def shift(array, axis, by):
        count = lax.axis_size(axis)
        return lax.ppermute(array, axis, [(i, i + by) for i in range(count) if 0 <= i + by < count])

    sent = register(recording, group_ids, shifts, first, tiles)
    arrived = lax.all_to_all(sent, "frames", 0, 0)
    arrived = arrived.reshape(-1, *arrived.shape[2:])
    ends, low_ends, high_ends, up, down = filter_cells(arrived, fir_taps, 0)
    below, above = shift(up, "frames", 1), shift(down, "frames", -1)
    slabs_ends = [shift(high_ends, "gz", 1), shift(low_ends, "gz", -1)]
    middle, low_middle, high_middle = filter_cells(arrived, fir_taps, 1)
    slabs_middle = [shift(high_middle, "gz", 1), shift(low_middle, "gz", -1)]
    image, part = inner(ends, middle, slabs_ends, slabs_middle, tile)
    part, below, above = lax.optimization_barrier((part, below, above))
    corners = []
    for at, by in ((planes - RADIUS, 1), (0, -1)):
        both = jnp.concatenate([below[at : at + RADIUS], above[at : at + RADIUS]], axis=1)
        corners.append(shift(both, "gz", by))
    return outer(ends, part, image, below, above, corners)


def solution(mesh):
    placed = (P("frames", "gz", None, None), P(), P(), P())
    return jax.shard_map(
        body, mesh=mesh, in_specs=placed, out_specs=P("gz", "frames", None), check_vma=False
    )
```

```python
import functools

import jax
import jax.numpy as jnp
import numpy as np
from jax import lax
from jax.experimental import pallas as pl
from jax.experimental.pallas import tpu as pltpu
from jax.sharding import PartitionSpec as P

RADIUS = 3
EPSILON = 1e-05
SIGMA_XY = 1.5
SIGMA_Z = 1.0
HALF = 4
RUN = 16
PITCH = 24
VMEM = 24 * 1024 * 1024


def gaussian(sigma):
    offsets = np.arange(-RADIUS, RADIUS + 1).astype(np.float32)
    values = np.exp(-offsets * offsets / np.float32(2.0 * sigma * sigma)).astype(np.float32)
    return (values / values.sum(dtype=np.float32)).astype(np.float32)


KERNEL_X = gaussian(SIGMA_XY).astype(jnp.bfloat16).astype(np.float32)
KERNEL_Y = gaussian(SIGMA_XY)
KERNEL_Z = gaussian(SIGMA_Z)
CENTER = float(np.float32(np.float32(KERNEL_Z[RADIUS] * KERNEL_Y[RADIUS]) * KERNEL_X[RADIUS]))


COST = pl.CostEstimate(flops=1, bytes_accessed=1, transcendentals=0)


def params(*semantics):
    return pltpu.CompilerParams(dimension_semantics=semantics, vmem_limit_bytes=VMEM)


def register_kernel(slots, first_ref, groups_ref, shifts_ref, x_ref, out_ref, aligned):
    frame = pl.program_id(0)
    planes, rows, width = x_ref.shape[1:]
    cells = pl.ds(pl.multiple_of(pl.program_id(1) * 16, 16), 16)
    tile = rows // out_ref.shape[0]
    group = groups_ref[first_ref[0] + frame]
    shift_y, shift_x = shifts_ref[group, 0], shifts_ref[group, 1]
    lane = lax.broadcasted_iota(jnp.int32, (8, width), 1)
    upper = lax.broadcasted_iota(jnp.int32, (8, width), 0) < HALF
    back = shift_x > 0.0
    edge = jnp.where(back, 0, width - 1)
    roll = jnp.where(back, 1, width - 1)
    side_x = jnp.where(lane == edge, 0.0, jnp.abs(shift_x))[None]
    here_x = 1.0 - jnp.abs(shift_x)
    zeros = jnp.zeros((8, width), jnp.float32)
    step = min(128, rows)
    for plane in range(planes):
        aligned[plane, 0:8] = zeros
        aligned[plane, rows + 8 : rows + 16] = zeros
        for start in range(0, rows, step):
            values = x_ref[0, plane, start : start + step].astype(jnp.float32)
            moved = pltpu.roll(values, roll, 1).reshape(step // 8, 8, width)
            mixed = here_x * values.reshape(step // 8, 8, width) + side_x * moved
            aligned[plane, 8 + start : 8 + start + step] = mixed.reshape(step, width)
    here_y, side_y = 1.0 - jnp.abs(shift_y), jnp.abs(shift_y)

    def finish(offset):
        def unit(plane, row):
            here = aligned[plane, 8 + row : 16 + row]
            beside = aligned[plane, 8 + offset + row : 16 + offset + row]
            return here_y * here + side_y * beside

        before = [unit(plane, -HALF) for plane in range(planes)]
        for t in range(rows // tile):
            middle, ends = [], []
            for plane in range(planes):
                middle.append(unit(plane, t * tile + HALF))
                after = unit(plane, t * tile + tile - HALF)
                ends.append(jnp.where(upper, after, before[plane]))
                before[plane] = after
            out_ref[slots[t], frame, 0, cells] = jnp.concatenate(ends, axis=0).astype(out_ref.dtype)
            out_ref[slots[t], frame, 1, cells] = jnp.concatenate(middle, axis=0).astype(out_ref.dtype)

    pl.when(shift_y > 0.0)(lambda: finish(-1))
    pl.when(shift_y <= 0.0)(lambda: finish(1))


def register(recording, group_ids, shifts, first, slots):
    tiles = len(slots)
    frames, planes, rows, width = recording.shape
    smem = pl.BlockSpec(memory_space=pltpu.SMEM)
    return pl.pallas_call(
        functools.partial(register_kernel, slots),
        grid=(frames, planes // 2),
        in_specs=[smem, smem, smem, pl.BlockSpec((1, 2, rows, width), lambda f, j: (f, j, 0, 0))],
        out_specs=pl.BlockSpec(memory_space=pltpu.VMEM),
        out_shape=jax.ShapeDtypeStruct((tiles, frames, 2, planes * 8, width), recording.dtype),
        scratch_shapes=[pltpu.VMEM((2, rows + 16, width), jnp.float32)],
        cost_estimate=COST,
        compiler_params=params("arbitrary", "arbitrary"),
        name="register",
    )(first, group_ids, shifts, recording)


def filter_kernel(part, taps_ref, x_ref, *refs):
    matrix, rows = refs[-2:]
    out_ref, one, other = refs[-5:-2]
    frames, _, cells, width = x_ref.shape
    planes, tile = out_ref.shape[0], 16
    taps = taps_ref.shape[0]
    reach = (taps - 1) // 2
    t = lax.broadcasted_iota(jnp.int32, (frames, frames), 0)
    u = lax.broadcasted_iota(jnp.int32, (frames, frames), 1)
    distance = u - t + reach
    band = jnp.zeros((frames, frames), jnp.float32)
    for k in range(taps):
        band = jnp.where(distance == k, taps_ref[k], band)
    matrix[...] = (band / jnp.sum(band, axis=1, keepdims=True)).astype(matrix.dtype)

    @pl.loop(0, cells // tile)
    def _(step):
        at = pl.multiple_of(step * tile, tile)
        rows[:, :tile] = x_ref[:, part, pl.ds(at, tile)].astype(jnp.float32)
        flat = rows.reshape(frames * PITCH, width)
        weights = matrix[...]
        for cell in range(tile):
            values = flat[pl.ds(cell, frames, stride=PITCH), :]
            baseline = jnp.dot(weights, values.astype(jnp.bfloat16), preferred_element_type=jnp.float32)
            detrended = values - baseline
            average = jnp.sum(detrended, axis=0, keepdims=True) * (1.0 / frames)
            centred = detrended - average
            power = jnp.sum(centred * centred, axis=0, keepdims=True) * (1.0 / frames)
            plane, row = step * 2 + cell // 8, cell % 8
            normed = (centred * lax.rsqrt(power + EPSILON)).astype(out_ref.dtype)
            out_ref[plane, row] = normed
            if part == 0 and HALF - RADIUS <= row < HALF:
                one[plane, row - (HALF - RADIUS)] = normed
            if part == 0 and HALF <= row < HALF + RADIUS:
                other[plane, row - HALF] = normed

    if part == 1:
        ends = refs[0]
        for k in range(RADIUS):
            for slab, plane in ((one, planes - RADIUS + k), (other, k)):
                slab[k, :8] = ends[plane]
                slab[k, 8:] = out_ref[plane]


def filter_cells(registered, fir_taps, part, *before):
    frames, _, cells, width = registered.shape
    planes = cells // 8

    def shape(*size):
        return jax.ShapeDtypeStruct((*size, frames, width), registered.dtype)

    halo = shape(planes, RADIUS) if part == 0 else shape(RADIUS, 16)
    vmem = pl.BlockSpec(memory_space=pltpu.VMEM)
    return pl.pallas_call(
        functools.partial(filter_kernel, part),
        in_specs=[pl.BlockSpec(memory_space=pltpu.SMEM), vmem] + [vmem] * len(before),
        out_specs=[vmem] * 3,
        out_shape=[shape(planes, 8), halo, halo],
        scratch_shapes=[pltpu.VMEM((frames, frames), jnp.bfloat16), pltpu.VMEM((frames, PITCH, width), jnp.float32)],
        cost_estimate=COST,
        compiler_params=params(),
        name="filter",
    )(fir_taps, registered, *before)


def pair_sums(parts, taps):
    total = taps[RADIUS] * parts[RADIUS]
    for k in range(RADIUS):
        total = total + taps[k] * (parts[k] + parts[2 * RADIUS - k])
    return total


TAPS_Y = [float(v) for v in KERNEL_Y]
TAPS_Z = [float(v) for v in KERNEL_Z]
WINDOW = 2 * RADIUS + 1


def smooth_z(current, target):
    planes = target.shape[0]
    for start in range(0, current.shape[1], 16):
        parts = [current[z, start : start + 16].astype(jnp.float32) for z in range(planes + 2 * RADIUS)]
        for z in range(planes):
            target[z, start : start + 16] = pair_sums(parts[z : z + WINDOW], TAPS_Z)


def band_of(matrix):
    width = matrix.shape[0]
    distance = lax.broadcasted_iota(jnp.int32, (width, width), 1) - lax.broadcasted_iota(
        jnp.int32, (width, width), 0
    )
    band = jnp.zeros((width, width), jnp.float32)
    for k in range(WINDOW):
        band = jnp.where(distance == k - RADIUS, float(KERNEL_X[k]), band)
    matrix[...] = band.astype(matrix.dtype)


def row_of_image(mixed, values_of, matrix, out_ref, y):
    for z in range(mixed.shape[0]):
        smoothed = jnp.dot(mixed[z], matrix[...], preferred_element_type=jnp.float32)
        values = values_of(z).astype(jnp.float32)
        frames = values.shape[0]
        total = jnp.sum(values * (smoothed - CENTER * values), axis=0, keepdims=True)
        out_ref[z, pl.ds(y, 1), :] = total * (1.0 / (frames * (1.0 - CENTER)))


def inner_kernel(ends, middle, low, high, out_ref, part_ref, *scratch):
    current, ring, mixed, values, matrix = scratch
    planes, tile = out_ref.shape[0], out_ref.shape[1]
    frames = current.shape[1]
    band_of(matrix)
    for row in range(RADIUS):
        ring[row] = jnp.zeros(ring.shape[1:], ring.dtype)

    def take(y):
        inside = (y >= HALF) & (y < tile - HALF)
        row = jnp.where(inside, y - HALF, jnp.where(y < HALF, y + HALF, y - (tile - HALF)))

        beside = jnp.where(inside, 8, 0)

        def fill(own):
            for k in range(RADIUS):
                current[k] = low[k, row + beside]
                current[RADIUS + planes + k] = high[k, row + beside]
            for z in range(planes):
                current[RADIUS + z] = own[z, row]

        pl.when(inside)(lambda: fill(middle))
        pl.when(jnp.logical_not(inside))(lambda: fill(ends))
        smooth_z(current, ring.at[lax.rem(y + RADIUS, WINDOW)])

    def rows_of(y, z, start):
        return pair_sums([ring[lax.rem(y + k, WINDOW), z, start : start + 32] for k in range(WINDOW)], TAPS_Y)

    def give_part(y, at):
        for z in range(planes):
            for start in range(0, frames, 32):
                part_ref[at, z, start : start + 32] = rows_of(y, z, start)

    def give(y):
        inside = (y >= HALF) & (y < tile - HALF)
        row = jnp.where(inside, y - HALF, jnp.where(y < HALF, y + HALF, y - (tile - HALF)))

        def fill(own):
            for z in range(planes):
                values[z] = own[z, row]

        pl.when(inside)(lambda: fill(middle))
        pl.when(jnp.logical_not(inside))(lambda: fill(ends))
        for z in range(planes):
            for start in range(0, frames, 32):
                mixed[z, start : start + 32] = rows_of(y, z, start).astype(mixed.dtype)
        row_of_image(mixed, lambda z: values[z], matrix, out_ref, y)

    pl.loop(0, RADIUS)(take)

    @pl.loop(RADIUS, 2 * RADIUS)
    def _(y):
        take(y)
        give_part(y - RADIUS, y - RADIUS)

    @pl.loop(2 * RADIUS, tile)
    def _(y):
        take(y)
        give(y - RADIUS)

    @pl.loop(tile, tile + RADIUS)
    def _(y):
        slot = lax.rem(y + RADIUS, WINDOW)
        ring[slot] = jnp.zeros(ring.shape[1:], ring.dtype)
        give_part(y - RADIUS, y - tile + RADIUS)


def outer_kernel(ends, part, image, *refs):
    sides, (out_ref, current, halo, mixed, matrix) = refs[:-5], refs[-5:]
    planes, tile = out_ref.shape[0], out_ref.shape[1]
    frames = current.shape[1]
    band_of(matrix)
    out_ref[...] = image[...]

    def side(low, own, high, first, upper):
        @pl.loop(0, RADIUS)
        def _(k):
            for j in range(RADIUS):
                current[j] = low[j, first + k]
                current[RADIUS + planes + j] = high[j, first + k]
            for z in range(planes):
                current[RADIUS + z] = own[z, k]
            smooth_z(current, halo.at[k])

        for n in range(RADIUS):
            y = tile - RADIUS + n if upper else n
            taps = [((tile + k if upper else k - RADIUS) - y + RADIUS, k) for k in range(RADIUS)]
            taps = [(TAPS_Y[at], k) for at, k in taps if 0 <= at < WINDOW]
            for z in range(planes):
                for start in range(0, frames, 32):
                    total = part[n + RADIUS * upper, z, start : start + 32]
                    for tap, k in taps:
                        total = total + tap * halo[k, z, start : start + 32]
                    mixed[z, start : start + 32] = total.astype(mixed.dtype)
            row = y - (tile - HALF) if upper else y + HALF
            row_of_image(mixed, lambda z: ends[z, row], matrix, out_ref, y)

    below, above, low_corners, high_corners = sides
    side(low_corners, below, high_corners, 0, 0)
    side(low_corners, above, high_corners, RADIUS, 1)


def inner(ends, middle, slabs, tile):
    planes, _, frames, width = ends.shape
    vmem = pl.BlockSpec(memory_space=pltpu.VMEM)
    return pl.pallas_call(
        inner_kernel,
        in_specs=[vmem] * 4,
        out_specs=[vmem] * 2,
        out_shape=[
            jax.ShapeDtypeStruct((planes, tile, width), jnp.float32),
            jax.ShapeDtypeStruct((2 * RADIUS, planes, frames, width), jnp.float32),
        ],
        scratch_shapes=[
            pltpu.VMEM((planes + 2 * RADIUS, frames, width), jnp.bfloat16),
            pltpu.VMEM((WINDOW, planes, frames, width), jnp.float32),
            pltpu.VMEM((planes, frames, width), jnp.bfloat16),
            pltpu.VMEM((planes, frames, width), jnp.bfloat16),
            pltpu.VMEM((width, width), jnp.bfloat16),
        ],
        cost_estimate=COST,
        compiler_params=params(),
        name="inner",
    )(ends, middle, *slabs)


def outer(ends, part, image, below, above, corners):
    planes, _, frames, width = ends.shape
    vmem = pl.BlockSpec(memory_space=pltpu.VMEM)
    return pl.pallas_call(
        outer_kernel,
        in_specs=[vmem] * 7,
        out_specs=vmem,
        out_shape=jax.ShapeDtypeStruct(image.shape, jnp.float32),
        scratch_shapes=[
            pltpu.VMEM((planes + 2 * RADIUS, frames, width), jnp.bfloat16),
            pltpu.VMEM((RADIUS, planes, frames, width), jnp.float32),
            pltpu.VMEM((planes, frames, width), jnp.bfloat16),
            pltpu.VMEM((width, width), jnp.bfloat16),
        ],
        cost_estimate=COST,
        compiler_params=params(),
        name="outer",
    )(ends, part, image, below, above, *corners)


def body(recording, group_ids, shifts, fir_taps):
    planes, rows = recording.shape[1], recording.shape[2]
    tiles, slabs = lax.axis_size("frames"), lax.axis_size("gz")
    tile = rows // tiles
    first = (lax.axis_index("frames") * recording.shape[0]).reshape(1)

    slots = [t if t // RUN % 2 == 0 else t // RUN * RUN + RUN - 1 - t % RUN for t in range(tiles)]

    def shift(array, axis, by):
        places = slots if axis == "frames" else list(range(lax.axis_size(axis)))
        return lax.ppermute(array, axis, [(p, places[i + by]) for i, p in enumerate(places) if 0 <= i + by < len(places)])

    sent = register(recording, group_ids, shifts, first, slots)
    arrived = lax.all_to_all(sent, "frames", 0, 0)
    arrived = arrived.reshape(-1, *arrived.shape[2:])
    ends, up, down = filter_cells(arrived, fir_taps, 0)
    below, above = shift(up, "frames", 1), shift(down, "frames", -1)
    middle, to_next, to_last = filter_cells(arrived, fir_taps, 1, ends)
    slabs = [shift(to_next, "gz", 1), shift(to_last, "gz", -1)]
    image, part = inner(ends, middle, slabs, tile)
    corners = []
    for at, by in ((planes - RADIUS, 1), (0, -1)):
        both = jnp.concatenate([below[at : at + RADIUS], above[at : at + RADIUS]], axis=1)
        corners.append(shift(both, "gz", by))
    image = outer(ends, part, image, below, above, corners)
    return lax.ppermute(image, "frames", [(p, t) for t, p in enumerate(slots)])


def solution(mesh):
    placed = (P("frames", "gz", None, None), P(), P(), P())
    return jax.shard_map(
        body, mesh=mesh, in_specs=placed, out_specs=P("gz", "frames", None), check_vma=False
    )
```

```python
import functools

import jax
import jax.numpy as jnp
import numpy as np
from jax import lax
from jax.experimental import pallas as pl
from jax.experimental.pallas import tpu as pltpu
from jax.sharding import PartitionSpec as P

RADIUS = 3
EPSILON = 1e-05
SIGMA_XY = 1.5
SIGMA_Z = 1.0
HALF = 4
RUN = 16
PITCH = 24
VMEM = 24 * 1024 * 1024


def gaussian(sigma):
    offsets = np.arange(-RADIUS, RADIUS + 1).astype(np.float32)
    values = np.exp(-offsets * offsets / np.float32(2.0 * sigma * sigma)).astype(np.float32)
    return (values / values.sum(dtype=np.float32)).astype(np.float32)


KERNEL_X = gaussian(SIGMA_XY).astype(jnp.bfloat16).astype(np.float32)
KERNEL_Y = gaussian(SIGMA_XY)
KERNEL_Z = gaussian(SIGMA_Z)
CENTER = float(np.float32(np.float32(KERNEL_Z[RADIUS] * KERNEL_Y[RADIUS]) * KERNEL_X[RADIUS]))


COST = pl.CostEstimate(flops=1, bytes_accessed=1, transcendentals=0)


def params(*semantics):
    return pltpu.CompilerParams(dimension_semantics=semantics, vmem_limit_bytes=VMEM)


def register_kernel(slots, first_ref, groups_ref, shifts_ref, x_ref, out_ref, aligned):
    frame = pl.program_id(0)
    planes, rows, width = x_ref.shape[1:]
    cells = pl.ds(pl.multiple_of(pl.program_id(1) * 16, 16), 16)
    tile = rows // out_ref.shape[0]
    group = groups_ref[first_ref[0] + frame]
    shift_y, shift_x = shifts_ref[group, 0], shifts_ref[group, 1]
    lane = lax.broadcasted_iota(jnp.int32, (8, width), 1)
    upper = lax.broadcasted_iota(jnp.int32, (8, width), 0) < HALF
    back = shift_x > 0.0
    edge = jnp.where(back, 0, width - 1)
    roll = jnp.where(back, 1, width - 1)
    side_x = jnp.where(lane == edge, 0.0, jnp.abs(shift_x))[None]
    here_x = 1.0 - jnp.abs(shift_x)
    zeros = jnp.zeros((8, width), jnp.float32)
    step = min(128, rows)
    for plane in range(planes):
        aligned[plane, 0:8] = zeros
        aligned[plane, rows + 8 : rows + 16] = zeros
        for start in range(0, rows, step):
            values = x_ref[0, plane, start : start + step].astype(jnp.float32)
            moved = pltpu.roll(values, roll, 1).reshape(step // 8, 8, width)
            mixed = here_x * values.reshape(step // 8, 8, width) + side_x * moved
            aligned[plane, 8 + start : 8 + start + step] = mixed.reshape(step, width)
    here_y, side_y = 1.0 - jnp.abs(shift_y), jnp.abs(shift_y)

    def finish(offset):
        def unit(plane, row):
            here = aligned[plane, 8 + row : 16 + row]
            beside = aligned[plane, 8 + offset + row : 16 + offset + row]
            return here_y * here + side_y * beside

        before = [unit(plane, -HALF) for plane in range(planes)]
        for t in range(rows // tile):
            middle, ends = [], []
            for plane in range(planes):
                middle.append(unit(plane, t * tile + HALF))
                after = unit(plane, t * tile + tile - HALF)
                ends.append(jnp.where(upper, after, before[plane]))
                before[plane] = after
            out_ref[slots[t], frame, 0, cells] = jnp.concatenate(ends, axis=0).astype(out_ref.dtype)
            out_ref[slots[t], frame, 1, cells] = jnp.concatenate(middle, axis=0).astype(out_ref.dtype)

    pl.when(shift_y > 0.0)(lambda: finish(-1))
    pl.when(shift_y <= 0.0)(lambda: finish(1))


def register(recording, group_ids, shifts, first, slots):
    tiles = len(slots)
    frames, planes, rows, width = recording.shape
    smem = pl.BlockSpec(memory_space=pltpu.SMEM)
    return pl.pallas_call(
        functools.partial(register_kernel, slots),
        grid=(frames, planes // 2),
        in_specs=[smem, smem, smem, pl.BlockSpec((1, 2, rows, width), lambda f, j: (f, j, 0, 0))],
        out_specs=pl.BlockSpec(memory_space=pltpu.VMEM),
        out_shape=jax.ShapeDtypeStruct((tiles, frames, 2, planes * 8, width), recording.dtype),
        scratch_shapes=[pltpu.VMEM((2, rows + 16, width), jnp.float32)],
        cost_estimate=COST,
        compiler_params=params("arbitrary", "arbitrary"),
        name="register",
    )(first, group_ids, shifts, recording)


def filter_kernel(part, taps_ref, x_ref, *refs):
    matrix, rows = refs[-2:]
    out_ref, one, other = refs[-5:-2]
    frames, _, cells, width = x_ref.shape
    planes, tile = out_ref.shape[0], 16
    taps = taps_ref.shape[0]
    reach = (taps - 1) // 2
    t = lax.broadcasted_iota(jnp.int32, (frames, frames), 0)
    u = lax.broadcasted_iota(jnp.int32, (frames, frames), 1)
    distance = u - t + reach
    band = jnp.zeros((frames, frames), jnp.float32)
    for k in range(taps):
        band = jnp.where(distance == k, taps_ref[k], band)
    matrix[...] = (band / jnp.sum(band, axis=1, keepdims=True)).astype(matrix.dtype)

    @pl.loop(0, cells // tile)
    def _(step):
        at = pl.multiple_of(step * tile, tile)
        rows[:, :tile] = x_ref[:, part, pl.ds(at, tile)].astype(jnp.float32)
        flat = rows.reshape(frames * PITCH, width)
        weights = matrix[...]
        for cell in range(tile):
            values = flat[pl.ds(cell, frames, stride=PITCH), :]
            baseline = jnp.dot(weights, values.astype(jnp.bfloat16), preferred_element_type=jnp.float32)
            detrended = values - baseline
            average = jnp.sum(detrended, axis=0, keepdims=True) * (1.0 / frames)
            centred = detrended - average
            power = jnp.sum(centred * centred, axis=0, keepdims=True) * (1.0 / frames)
            plane, row = step * 2 + cell // 8, cell % 8
            normed = (centred * lax.rsqrt(power + EPSILON)).astype(out_ref.dtype)
            out_ref[plane, row] = normed
            if part == 0 and HALF - RADIUS <= row < HALF:
                one[plane, row - (HALF - RADIUS)] = normed
            if part == 0 and HALF <= row < HALF + RADIUS:
                other[plane, row - HALF] = normed

    if part == 1:
        ends = refs[0]
        for k in range(RADIUS):
            for slab, plane in ((one, planes - RADIUS + k), (other, k)):
                slab[k, :8] = ends[plane]
                slab[k, 8:] = out_ref[plane]


def filter_cells(registered, fir_taps, part, *before):
    frames, _, cells, width = registered.shape
    planes = cells // 8

    def shape(*size):
        return jax.ShapeDtypeStruct((*size, frames, width), registered.dtype)

    halo = shape(planes, RADIUS) if part == 0 else shape(RADIUS, 16)
    vmem = pl.BlockSpec(memory_space=pltpu.VMEM)
    return pl.pallas_call(
        functools.partial(filter_kernel, part),
        in_specs=[pl.BlockSpec(memory_space=pltpu.SMEM), vmem] + [vmem] * len(before),
        out_specs=[vmem] * 3,
        out_shape=[shape(planes, 8), halo, halo],
        scratch_shapes=[pltpu.VMEM((frames, frames), jnp.bfloat16), pltpu.VMEM((frames, PITCH, width), jnp.float32)],
        cost_estimate=COST,
        compiler_params=params(),
        name="filter",
    )(fir_taps, registered, *before)


def pair_sums(parts, taps):
    total = parts[RADIUS]
    for k in range(RADIUS):
        total = total + taps[k] * (parts[k] + parts[2 * RADIUS - k])
    return total


TAPS_Y = [float(v / KERNEL_Y[RADIUS]) for v in KERNEL_Y]
TAPS_Z = [float(v / KERNEL_Z[RADIUS]) for v in KERNEL_Z]
SCALE = float(KERNEL_Z[RADIUS]) * float(KERNEL_Y[RADIUS])
WINDOW = 2 * RADIUS + 1


def smooth_z(rows, target):
    planes, frames = target.shape[0], target.shape[1]
    for start in range(0, frames, 16):
        parts = [ref[z, row, start : start + 16].astype(jnp.float32) for ref, z, row in rows]
        for z in range(planes):
            target[z, start : start + 16] = pair_sums(parts[z : z + WINDOW], TAPS_Z)


def stack(low, own, high, planes, low_row, own_row, high_row):
    rows = [(low, k, low_row) for k in range(RADIUS)]
    rows += [(own, z, own_row) for z in range(planes)]
    return rows + [(high, k, high_row) for k in range(RADIUS)]


def band_of(matrix):
    width = matrix.shape[1]
    distance = lax.broadcasted_iota(jnp.int32, (width, width), 1) - lax.broadcasted_iota(
        jnp.int32, (width, width), 0
    )
    band = jnp.zeros((width, width), jnp.float32)
    for k in range(WINDOW):
        band = jnp.where(distance == k - RADIUS, float(KERNEL_X[k]), band)
    matrix[:width] = band.astype(matrix.dtype)
    matrix[width:] = jnp.where(distance == 0, -float(KERNEL_X[RADIUS]), 0.0).astype(matrix.dtype)


def row_of_image(mixed, values_of, matrix, out_ref, y):
    for z in range(mixed.shape[0]):
        values = values_of(z)
        both = jnp.concatenate([mixed[z], values], axis=1)
        neighbor = jnp.dot(both, matrix[...], preferred_element_type=jnp.float32)
        total = jnp.sum(values.astype(jnp.float32) * neighbor, axis=0, keepdims=True)
        out_ref[z, pl.ds(y, 1), :] = total * (SCALE / (values.shape[0] * (1.0 - CENTER)))


def inner_kernel(ends, middle, low, high, out_ref, part_ref, *scratch):
    ring, mixed, matrix = scratch
    planes, tile = out_ref.shape[0], out_ref.shape[1]
    frames = ring.shape[2]
    band_of(matrix)
    for row in range(RADIUS):
        ring[row] = jnp.zeros(ring.shape[1:], ring.dtype)

    def first_ends(y):
        return ends, y + HALF, y + HALF

    def inside(y):
        return middle, y - HALF, y + HALF

    def last_ends(y):
        return ends, y - (tile - HALF), y - (tile - HALF)

    def slot(y):
        return lax.rem(y + RADIUS, ring.shape[0])

    def take(y, where):
        own, row, beside = where(y)
        smooth_z(stack(low, own, high, planes, beside, row, beside), ring.at[slot(y)])

    def give_part(y, at):
        for z in range(planes):
            for start in range(0, frames, 32):
                parts = [ring[slot(y + k - RADIUS), z, start : start + 32] for k in range(WINDOW)]
                part_ref[at, z, start : start + 32] = pair_sums(parts, TAPS_Y)

    def give_two(y, *where):
        for z in range(planes):
            for start in range(0, frames, 32):
                parts = [ring[slot(y + k - RADIUS), z, start : start + 32] for k in range(WINDOW + 1)]
                for n in range(2):
                    total = pair_sums(parts[n : n + WINDOW], TAPS_Y)
                    mixed[n, z, start : start + 32] = total.astype(mixed.dtype)
        for n in range(2):
            own, row, _ = where[n](y + n)
            row_of_image(mixed.at[n], lambda z, own=own, row=row: own[z, row], matrix, out_ref, y + n)

    def run(begin, end, taken, *given):
        @pl.loop(0, (end - begin) // 2)
        def _(i):
            y = begin + 2 * i
            take(y, taken)
            take(y + 1, taken)
            if given:
                give_two(y - RADIUS, *given)

    turn = tile - HALF
    pl.loop(0, RADIUS)(lambda y: take(y, first_ends))

    @pl.loop(RADIUS, 2 * RADIUS)
    def _(y):
        pl.when(y < HALF)(lambda: take(y, first_ends))
        pl.when(y >= HALF)(lambda: take(y, inside))
        give_part(y - RADIUS, y - RADIUS)

    run(2 * RADIUS, 2 * RADIUS + 2, inside, first_ends, inside)
    run(2 * RADIUS + 2, turn, inside, inside, inside)
    run(turn, turn + 2, last_ends, inside, inside)
    run(turn + 2, tile, last_ends, inside, last_ends)

    @pl.loop(tile, tile + RADIUS)
    def _(y):
        ring[slot(y)] = jnp.zeros(ring.shape[1:], ring.dtype)
        give_part(y - RADIUS, y - tile + RADIUS)


def outer_kernel(ends, part, image, *refs):
    sides, (out_ref, halo, mixed, matrix) = refs[:-4], refs[-4:]
    planes, tile = out_ref.shape[0], out_ref.shape[1]
    frames = halo.shape[2]
    band_of(matrix)
    out_ref[...] = image[...]

    def side(low, own, high, first, upper):
        @pl.loop(0, RADIUS)
        def _(k):
            smooth_z(stack(low, own, high, planes, first + k, k, first + k), halo.at[k])

        for n in range(RADIUS):
            y = tile - RADIUS + n if upper else n
            taps = [((tile + k if upper else k - RADIUS) - y + RADIUS, k) for k in range(RADIUS)]
            taps = [(TAPS_Y[at], k) for at, k in taps if 0 <= at < WINDOW]
            for z in range(planes):
                for start in range(0, frames, 32):
                    total = part[n + RADIUS * upper, z, start : start + 32]
                    for tap, k in taps:
                        total = total + tap * halo[k, z, start : start + 32]
                    mixed[z, start : start + 32] = total.astype(mixed.dtype)
            row = y - (tile - HALF) if upper else y + HALF
            row_of_image(mixed, lambda z: ends[z, row], matrix, out_ref, y)

    below, above, low_corners, high_corners = sides
    side(low_corners, below, high_corners, 0, 0)
    side(low_corners, above, high_corners, RADIUS, 1)


def inner(ends, middle, slabs, tile):
    planes, _, frames, width = ends.shape
    vmem = pl.BlockSpec(memory_space=pltpu.VMEM)
    return pl.pallas_call(
        inner_kernel,
        in_specs=[vmem] * 4,
        out_specs=[vmem] * 2,
        out_shape=[
            jax.ShapeDtypeStruct((planes, tile, width), jnp.float32),
            jax.ShapeDtypeStruct((2 * RADIUS, planes, frames, width), jnp.float32),
        ],
        scratch_shapes=[
            pltpu.VMEM((WINDOW + 1, planes, frames, width), jnp.float32),
            pltpu.VMEM((2, planes, frames, width), jnp.bfloat16),
            pltpu.VMEM((2 * width, width), jnp.bfloat16),
        ],
        cost_estimate=COST,
        compiler_params=params(),
        name="inner",
    )(ends, middle, *slabs)


def outer(ends, part, image, below, above, corners):
    planes, _, frames, width = ends.shape
    vmem = pl.BlockSpec(memory_space=pltpu.VMEM)
    return pl.pallas_call(
        outer_kernel,
        in_specs=[vmem] * 7,
        out_specs=vmem,
        out_shape=jax.ShapeDtypeStruct(image.shape, jnp.float32),
        scratch_shapes=[
            pltpu.VMEM((RADIUS, planes, frames, width), jnp.float32),
            pltpu.VMEM((planes, frames, width), jnp.bfloat16),
            pltpu.VMEM((2 * width, width), jnp.bfloat16),
        ],
        cost_estimate=COST,
        compiler_params=params(),
        name="outer",
    )(ends, part, image, below, above, *corners)


def body(recording, group_ids, shifts, fir_taps):
    planes, rows = recording.shape[1], recording.shape[2]
    tiles, slabs = lax.axis_size("frames"), lax.axis_size("gz")
    tile = rows // tiles
    first = (lax.axis_index("frames") * recording.shape[0]).reshape(1)

    slots = [t if t // RUN % 2 == 0 else t // RUN * RUN + RUN - 1 - t % RUN for t in range(tiles)]

    def shift(array, axis, by):
        places = slots if axis == "frames" else list(range(lax.axis_size(axis)))
        return lax.ppermute(array, axis, [(p, places[i + by]) for i, p in enumerate(places) if 0 <= i + by < len(places)])

    sent = register(recording, group_ids, shifts, first, slots)
    arrived = lax.all_to_all(sent, "frames", 0, 0)
    arrived = arrived.reshape(-1, *arrived.shape[2:])
    ends, up, down = filter_cells(arrived, fir_taps, 0)
    below, above = shift(up, "frames", 1), shift(down, "frames", -1)
    middle, to_next, to_last = filter_cells(arrived, fir_taps, 1, ends)
    slabs = [shift(to_next, "gz", 1), shift(to_last, "gz", -1)]
    image, part = inner(ends, middle, slabs, tile)
    corners = []
    for at, by in ((planes - RADIUS, 1), (0, -1)):
        both = jnp.concatenate([below[at : at + RADIUS], above[at : at + RADIUS]], axis=1)
        corners.append(shift(both, "gz", by))
    image = outer(ends, part, image, below, above, corners)
    return lax.ppermute(image, "frames", [(p, t) for t, p in enumerate(slots)])


def solution(mesh):
    placed = (P("frames", "gz", None, None), P(), P(), P())
    return jax.shard_map(
        body, mesh=mesh, in_specs=placed, out_specs=P("gz", "frames", None), check_vma=False
    )
```

```python
import functools

import jax
import jax.numpy as jnp
import numpy as np
from jax import lax
from jax.experimental import pallas as pl
from jax.experimental.pallas import tpu as pltpu
from jax.sharding import PartitionSpec as P

RADIUS = 3
EPSILON = 1e-05
SIGMA_XY = 1.5
SIGMA_Z = 1.0
HALF = 4
RUN = 16
PITCH = 24
VMEM = 24 * 1024 * 1024


def gaussian(sigma):
    offsets = np.arange(-RADIUS, RADIUS + 1).astype(np.float32)
    values = np.exp(-offsets * offsets / np.float32(2.0 * sigma * sigma)).astype(np.float32)
    return (values / values.sum(dtype=np.float32)).astype(np.float32)


KERNEL_X = gaussian(SIGMA_XY).astype(jnp.bfloat16).astype(np.float32)
KERNEL_Y = gaussian(SIGMA_XY)
KERNEL_Z = gaussian(SIGMA_Z)
CENTER = float(np.float32(np.float32(KERNEL_Z[RADIUS] * KERNEL_Y[RADIUS]) * KERNEL_X[RADIUS]))


COST = pl.CostEstimate(flops=1, bytes_accessed=1, transcendentals=0)


def params(*semantics):
    return pltpu.CompilerParams(dimension_semantics=semantics, vmem_limit_bytes=VMEM)


def register_kernel(slots, first_ref, groups_ref, shifts_ref, x_ref, out_ref, aligned):
    frame = pl.program_id(0)
    planes, rows, width = x_ref.shape[1:]
    cells = pl.ds(pl.multiple_of(pl.program_id(1) * 16, 16), 16)
    tile = rows // out_ref.shape[0]
    group = groups_ref[first_ref[0] + frame]
    shift_y, shift_x = shifts_ref[group, 0], shifts_ref[group, 1]
    lane = lax.broadcasted_iota(jnp.int32, (8, width), 1)
    upper = lax.broadcasted_iota(jnp.int32, (8, width), 0) < HALF
    back = shift_x > 0.0
    edge = jnp.where(back, 0, width - 1)
    roll = jnp.where(back, 1, width - 1)
    side_x = jnp.where(lane == edge, 0.0, jnp.abs(shift_x))[None]
    here_x = 1.0 - jnp.abs(shift_x)
    zeros = jnp.zeros((8, width), jnp.float32)
    step = min(128, rows)
    for plane in range(planes):
        aligned[plane, 0:8] = zeros
        aligned[plane, rows + 8 : rows + 16] = zeros
        for start in range(0, rows, step):
            values = x_ref[0, plane, start : start + step].astype(jnp.float32)
            moved = pltpu.roll(values, roll, 1).reshape(step // 8, 8, width)
            mixed = here_x * values.reshape(step // 8, 8, width) + side_x * moved
            aligned[plane, 8 + start : 8 + start + step] = mixed.reshape(step, width)
    here_y, side_y = 1.0 - jnp.abs(shift_y), jnp.abs(shift_y)

    def finish(offset):
        def unit(plane, row):
            here = aligned[plane, 8 + row : 16 + row]
            beside = aligned[plane, 8 + offset + row : 16 + offset + row]
            return here_y * here + side_y * beside

        before = [unit(plane, -HALF) for plane in range(planes)]
        for t in range(rows // tile):
            middle, ends = [], []
            for plane in range(planes):
                middle.append(unit(plane, t * tile + HALF))
                after = unit(plane, t * tile + tile - HALF)
                ends.append(jnp.where(upper, after, before[plane]))
                before[plane] = after
            out_ref[slots[t], frame, 0, cells] = jnp.concatenate(ends, axis=0).astype(out_ref.dtype)
            out_ref[slots[t], frame, 1, cells] = jnp.concatenate(middle, axis=0).astype(out_ref.dtype)

    pl.when(shift_y > 0.0)(lambda: finish(-1))
    pl.when(shift_y <= 0.0)(lambda: finish(1))


def register(recording, group_ids, shifts, first, slots):
    tiles = len(slots)
    frames, planes, rows, width = recording.shape
    smem = pl.BlockSpec(memory_space=pltpu.SMEM)
    return pl.pallas_call(
        functools.partial(register_kernel, slots),
        grid=(frames, planes // 2),
        in_specs=[smem, smem, smem, pl.BlockSpec((1, 2, rows, width), lambda f, j: (f, j, 0, 0))],
        out_specs=pl.BlockSpec(memory_space=pltpu.VMEM),
        out_shape=jax.ShapeDtypeStruct((tiles, frames, 2, planes * 8, width), recording.dtype),
        scratch_shapes=[pltpu.VMEM((2, rows + 16, width), jnp.float32)],
        cost_estimate=COST,
        compiler_params=params("arbitrary", "arbitrary"),
        name="register",
    )(first, group_ids, shifts, recording)


def filter_kernel(part, taps_ref, x_ref, *refs):
    matrix, rows = refs[-2:]
    out_ref, one, other = refs[-5:-2]
    frames, _, cells, width = x_ref.shape
    planes, tile = out_ref.shape[0], 16
    taps = taps_ref.shape[0]
    reach = (taps - 1) // 2
    t = lax.broadcasted_iota(jnp.int32, (frames, frames), 0)
    u = lax.broadcasted_iota(jnp.int32, (frames, frames), 1)
    distance = u - t + reach
    band = jnp.zeros((frames, frames), jnp.float32)
    for k in range(taps):
        band = jnp.where(distance == k, taps_ref[k], band)
    matrix[...] = (band / jnp.sum(band, axis=1, keepdims=True)).astype(matrix.dtype)

    @pl.loop(0, cells // tile)
    def _(step):
        at = pl.multiple_of(step * tile, tile)
        rows[:frames, :tile] = x_ref[:, part, pl.ds(at, tile)].astype(jnp.float32)
        flat = rows.reshape((frames + 1) * PITCH, width)
        weights = matrix[...]
        for cell in range(tile):
            values = flat[pl.ds(cell, frames, stride=PITCH), :]
            baseline = jnp.dot(weights, values.astype(jnp.bfloat16), preferred_element_type=jnp.float32)
            detrended = values - baseline
            average = jnp.sum(detrended, axis=0, keepdims=True) * (1.0 / frames)
            centred = detrended - average
            power = jnp.sum(centred * centred, axis=0, keepdims=True) * (1.0 / frames)
            plane, row = step * 2 + cell // 8, cell % 8
            normed = (centred * lax.rsqrt(power + EPSILON)).astype(out_ref.dtype)
            out_ref[plane, row] = normed
            if part == 0 and HALF - RADIUS <= row < HALF:
                one[plane, row - (HALF - RADIUS)] = normed
            if part == 0 and HALF <= row < HALF + RADIUS:
                other[plane, row - HALF] = normed

    if part == 1:
        ends = refs[0]
        for k in range(RADIUS):
            for slab, plane in ((one, planes - RADIUS + k), (other, k)):
                slab[k, :8] = ends[plane]
                slab[k, 8:] = out_ref[plane]


def filter_cells(registered, fir_taps, part, *before):
    frames, _, cells, width = registered.shape
    planes = cells // 8

    def shape(*size):
        return jax.ShapeDtypeStruct((*size, frames, width), registered.dtype)

    halo = shape(planes, RADIUS) if part == 0 else shape(RADIUS, 16)
    vmem = pl.BlockSpec(memory_space=pltpu.VMEM)
    return pl.pallas_call(
        functools.partial(filter_kernel, part),
        in_specs=[pl.BlockSpec(memory_space=pltpu.SMEM), vmem] + [vmem] * len(before),
        out_specs=[vmem] * 3,
        out_shape=[shape(planes, 8), halo, halo],
        scratch_shapes=[pltpu.VMEM((frames, frames), jnp.bfloat16), pltpu.VMEM((frames + 1, PITCH, width), jnp.float32)],
        cost_estimate=COST,
        compiler_params=params(),
        name="filter",
    )(fir_taps, registered, *before)


def pair_sums(parts, taps):
    total = parts[RADIUS]
    for k in range(RADIUS):
        total = total + taps[k] * (parts[k] + parts[2 * RADIUS - k])
    return total


TAPS_Y = [float(v / KERNEL_Y[RADIUS]) for v in KERNEL_Y]
TAPS_Z = [float(v / KERNEL_Z[RADIUS]) for v in KERNEL_Z]
SCALE = float(KERNEL_Z[RADIUS]) * float(KERNEL_Y[RADIUS])
WINDOW = 2 * RADIUS + 1


def smooth_z(rows, target):
    planes, frames = target.shape[0], target.shape[1]
    for start in range(0, frames, 16):
        parts = [ref[z, row, start : start + 16].astype(jnp.float32) for ref, z, row in rows]
        for z in range(planes):
            target[z, start : start + 16] = pair_sums(parts[z : z + WINDOW], TAPS_Z)


def stack(low, own, high, planes, low_row, own_row, high_row):
    rows = [(low, k, low_row) for k in range(RADIUS)]
    rows += [(own, z, own_row) for z in range(planes)]
    return rows + [(high, k, high_row) for k in range(RADIUS)]


def band_of(matrix):
    width = matrix.shape[1]
    distance = lax.broadcasted_iota(jnp.int32, (width, width), 1) - lax.broadcasted_iota(
        jnp.int32, (width, width), 0
    )
    band = jnp.zeros((width, width), jnp.float32)
    for k in range(WINDOW):
        band = jnp.where(distance == k - RADIUS, float(KERNEL_X[k]), band)
    matrix[:width] = band.astype(matrix.dtype)
    matrix[width:] = jnp.where(distance == 0, -float(KERNEL_X[RADIUS]), 0.0).astype(matrix.dtype)


def row_of_image(mixed, values_of, matrix, out_ref, y):
    for z in range(mixed.shape[0]):
        values = values_of(z)
        both = jnp.concatenate([mixed[z], values], axis=1)
        neighbor = jnp.dot(both, matrix[...], preferred_element_type=jnp.float32)
        total = jnp.sum(values.astype(jnp.float32) * neighbor, axis=0, keepdims=True)
        out_ref[z, pl.ds(y, 1), :] = total * (SCALE / (values.shape[0] * (1.0 - CENTER)))


def inner_kernel(ends, middle, low, high, out_ref, part_ref, *scratch):
    ring, mixed, matrix = scratch
    planes, tile = out_ref.shape[0], out_ref.shape[1]
    frames = ring.shape[2]
    band_of(matrix)
    for row in range(RADIUS):
        ring[row] = jnp.zeros(ring.shape[1:], ring.dtype)

    def first_ends(y):
        return ends, y + HALF, y + HALF

    def inside(y):
        return middle, y - HALF, y + HALF

    def last_ends(y):
        return ends, y - (tile - HALF), y - (tile - HALF)

    def slot(y):
        return lax.rem(y + RADIUS, ring.shape[0])

    def take(y, where):
        own, row, beside = where(y)
        smooth_z(stack(low, own, high, planes, beside, row, beside), ring.at[slot(y)])

    def give_part(y, at):
        for z in range(planes):
            for start in range(0, frames, 32):
                parts = [ring[slot(y + k - RADIUS), z, start : start + 32] for k in range(WINDOW)]
                part_ref[at, z, start : start + 32] = pair_sums(parts, TAPS_Y)

    def give_two(y, *where):
        for z in range(planes):
            for start in range(0, frames, 32):
                parts = [ring[slot(y + k - RADIUS), z, start : start + 32] for k in range(WINDOW + 1)]
                for n in range(2):
                    total = pair_sums(parts[n : n + WINDOW], TAPS_Y)
                    mixed[n, z, start : start + 32] = total.astype(mixed.dtype)
        for n in range(2):
            own, row, _ = where[n](y + n)
            row_of_image(mixed.at[n], lambda z, own=own, row=row: own[z, row], matrix, out_ref, y + n)

    def run(begin, end, taken, *given):
        @pl.loop(0, (end - begin) // 2)
        def _(i):
            y = begin + 2 * i
            take(y, taken)
            take(y + 1, taken)
            if given:
                give_two(y - RADIUS, *given)

    turn = tile - HALF
    pl.loop(0, RADIUS)(lambda y: take(y, first_ends))

    @pl.loop(RADIUS, 2 * RADIUS)
    def _(y):
        pl.when(y < HALF)(lambda: take(y, first_ends))
        pl.when(y >= HALF)(lambda: take(y, inside))
        give_part(y - RADIUS, y - RADIUS)

    run(2 * RADIUS, 2 * RADIUS + 2, inside, first_ends, inside)
    run(2 * RADIUS + 2, turn, inside, inside, inside)
    run(turn, turn + 2, last_ends, inside, inside)
    run(turn + 2, tile, last_ends, inside, last_ends)

    @pl.loop(tile, tile + RADIUS)
    def _(y):
        ring[slot(y)] = jnp.zeros(ring.shape[1:], ring.dtype)
        give_part(y - RADIUS, y - tile + RADIUS)


def outer_kernel(ends, part, image, *refs):
    sides, (out_ref, halo, mixed, matrix) = refs[:-4], refs[-4:]
    planes, tile = out_ref.shape[0], out_ref.shape[1]
    frames = halo.shape[2]
    band_of(matrix)
    out_ref[...] = image[...]

    def side(low, own, high, first, upper):
        @pl.loop(0, RADIUS)
        def _(k):
            smooth_z(stack(low, own, high, planes, first + k, k, first + k), halo.at[k])

        for n in range(RADIUS):
            y = tile - RADIUS + n if upper else n
            taps = [((tile + k if upper else k - RADIUS) - y + RADIUS, k) for k in range(RADIUS)]
            taps = [(TAPS_Y[at], k) for at, k in taps if 0 <= at < WINDOW]
            for z in range(planes):
                for start in range(0, frames, 32):
                    total = part[n + RADIUS * upper, z, start : start + 32]
                    for tap, k in taps:
                        total = total + tap * halo[k, z, start : start + 32]
                    mixed[z, start : start + 32] = total.astype(mixed.dtype)
            row = y - (tile - HALF) if upper else y + HALF
            row_of_image(mixed, lambda z: ends[z, row], matrix, out_ref, y)

    below, above, low_corners, high_corners = sides
    side(low_corners, below, high_corners, 0, 0)
    side(low_corners, above, high_corners, RADIUS, 1)


def inner(ends, middle, slabs, tile):
    planes, _, frames, width = ends.shape
    vmem = pl.BlockSpec(memory_space=pltpu.VMEM)
    return pl.pallas_call(
        inner_kernel,
        in_specs=[vmem] * 4,
        out_specs=[vmem] * 2,
        out_shape=[
            jax.ShapeDtypeStruct((planes, tile, width), jnp.float32),
            jax.ShapeDtypeStruct((2 * RADIUS, planes, frames, width), jnp.float32),
        ],
        scratch_shapes=[
            pltpu.VMEM((WINDOW + 1, planes, frames, width), jnp.float32),
            pltpu.VMEM((2, planes, frames, width), jnp.bfloat16),
            pltpu.VMEM((2 * width, width), jnp.bfloat16),
        ],
        cost_estimate=COST,
        compiler_params=params(),
        name="inner",
    )(ends, middle, *slabs)


def outer(ends, part, image, below, above, corners):
    planes, _, frames, width = ends.shape
    vmem = pl.BlockSpec(memory_space=pltpu.VMEM)
    return pl.pallas_call(
        outer_kernel,
        in_specs=[vmem] * 7,
        out_specs=vmem,
        out_shape=jax.ShapeDtypeStruct(image.shape, jnp.float32),
        scratch_shapes=[
            pltpu.VMEM((RADIUS, planes, frames, width), jnp.float32),
            pltpu.VMEM((planes, frames, width), jnp.bfloat16),
            pltpu.VMEM((2 * width, width), jnp.bfloat16),
        ],
        cost_estimate=COST,
        compiler_params=params(),
        name="outer",
    )(ends, part, image, below, above, *corners)


def body(recording, group_ids, shifts, fir_taps):
    planes, rows = recording.shape[1], recording.shape[2]
    tiles, slabs = lax.axis_size("frames"), lax.axis_size("gz")
    tile = rows // tiles
    first = (lax.axis_index("frames") * recording.shape[0]).reshape(1)

    slots = [t if t // RUN % 2 == 0 else t // RUN * RUN + RUN - 1 - t % RUN for t in range(tiles)]

    def shift(array, axis, by):
        places = slots if axis == "frames" else list(range(lax.axis_size(axis)))
        return lax.ppermute(array, axis, [(p, places[i + by]) for i, p in enumerate(places) if 0 <= i + by < len(places)])

    sent = register(recording, group_ids, shifts, first, slots)
    arrived = lax.all_to_all(sent, "frames", 0, 0)
    arrived = arrived.reshape(-1, *arrived.shape[2:])
    ends, up, down = filter_cells(arrived, fir_taps, 0)
    below, above = shift(up, "frames", 1), shift(down, "frames", -1)
    middle, to_next, to_last = filter_cells(arrived, fir_taps, 1, ends)
    slabs = [shift(to_next, "gz", 1), shift(to_last, "gz", -1)]
    image, part = inner(ends, middle, slabs, tile)
    corners = []
    for at, by in ((planes - RADIUS, 1), (0, -1)):
        both = jnp.concatenate([below[at : at + RADIUS], above[at : at + RADIUS]], axis=1)
        corners.append(shift(both, "gz", by))
    image = outer(ends, part, image, below, above, corners)
    return lax.ppermute(image, "frames", [(p, t) for t, p in enumerate(slots)])


def solution(mesh):
    placed = (P("frames", "gz", None, None), P(), P(), P())
    return jax.shard_map(
        body, mesh=mesh, in_specs=placed, out_specs=P("gz", "frames", None), check_vma=False
    )
```

```python
import functools

import jax
import jax.numpy as jnp
import numpy as np
from jax import lax
from jax.experimental import pallas as pl
from jax.experimental.pallas import tpu as pltpu
from jax.sharding import PartitionSpec as P

RADIUS = 3
EPSILON = 1e-05
SIGMA_XY = 1.5
SIGMA_Z = 1.0
HALF = 4
RUN = 16
PITCH = 24
VMEM = 24 * 1024 * 1024


def gaussian(sigma):
    offsets = np.arange(-RADIUS, RADIUS + 1).astype(np.float32)
    values = np.exp(-offsets * offsets / np.float32(2.0 * sigma * sigma)).astype(np.float32)
    return (values / values.sum(dtype=np.float32)).astype(np.float32)


KERNEL_X = gaussian(SIGMA_XY).astype(jnp.bfloat16).astype(np.float32)
KERNEL_Y = gaussian(SIGMA_XY)
KERNEL_Z = gaussian(SIGMA_Z)
CENTER = float(np.float32(np.float32(KERNEL_Z[RADIUS] * KERNEL_Y[RADIUS]) * KERNEL_X[RADIUS]))


COST = pl.CostEstimate(flops=1, bytes_accessed=1, transcendentals=0)


def params(*semantics):
    return pltpu.CompilerParams(dimension_semantics=semantics, vmem_limit_bytes=VMEM)


def register_kernel(slots, first_ref, groups_ref, shifts_ref, x_ref, out_ref, aligned):
    frame = pl.program_id(0)
    planes, rows, width = x_ref.shape[1:]
    cells = pl.ds(pl.multiple_of(pl.program_id(1) * 16, 16), 16)
    tile = rows // out_ref.shape[0]
    group = groups_ref[first_ref[0] + frame]
    shift_y, shift_x = shifts_ref[group, 0], shifts_ref[group, 1]
    lane = lax.broadcasted_iota(jnp.int32, (8, width), 1)
    upper = lax.broadcasted_iota(jnp.int32, (8, width), 0) < HALF
    back = shift_x > 0.0
    edge = jnp.where(back, 0, width - 1)
    roll = jnp.where(back, 1, width - 1)
    side_x = jnp.where(lane == edge, 0.0, jnp.abs(shift_x))[None]
    here_x = 1.0 - jnp.abs(shift_x)
    zeros = jnp.zeros((8, width), jnp.float32)
    step = min(128, rows)
    for plane in range(planes):
        aligned[plane, 0:8] = zeros
        aligned[plane, rows + 8 : rows + 16] = zeros
        for start in range(0, rows, step):
            values = x_ref[0, plane, start : start + step].astype(jnp.float32)
            moved = pltpu.roll(values, roll, 1).reshape(step // 8, 8, width)
            mixed = here_x * values.reshape(step // 8, 8, width) + side_x * moved
            aligned[plane, 8 + start : 8 + start + step] = mixed.reshape(step, width)
    here_y, side_y = 1.0 - jnp.abs(shift_y), jnp.abs(shift_y)

    def finish(offset):
        def unit(plane, row):
            here = aligned[plane, 8 + row : 16 + row]
            beside = aligned[plane, 8 + offset + row : 16 + offset + row]
            return here_y * here + side_y * beside

        before = [unit(plane, -HALF) for plane in range(planes)]
        for t in range(rows // tile):
            middle, ends = [], []
            for plane in range(planes):
                middle.append(unit(plane, t * tile + HALF))
                after = unit(plane, t * tile + tile - HALF)
                ends.append(jnp.where(upper, after, before[plane]))
                before[plane] = after
            out_ref[slots[t], frame, 0, cells] = jnp.concatenate(ends, axis=0).astype(out_ref.dtype)
            out_ref[slots[t], frame, 1, cells] = jnp.concatenate(middle, axis=0).astype(out_ref.dtype)

    pl.when(shift_y > 0.0)(lambda: finish(-1))
    pl.when(shift_y <= 0.0)(lambda: finish(1))


def register(recording, group_ids, shifts, first, slots):
    tiles = len(slots)
    frames, planes, rows, width = recording.shape
    smem = pl.BlockSpec(memory_space=pltpu.SMEM)
    return pl.pallas_call(
        functools.partial(register_kernel, slots),
        grid=(frames, planes // 2),
        in_specs=[smem, smem, smem, pl.BlockSpec((1, 2, rows, width), lambda f, j: (f, j, 0, 0))],
        out_specs=pl.BlockSpec(memory_space=pltpu.VMEM),
        out_shape=jax.ShapeDtypeStruct((tiles, frames, 2, planes * 8, width), recording.dtype),
        scratch_shapes=[pltpu.VMEM((2, rows + 16, width), jnp.float32)],
        cost_estimate=COST,
        compiler_params=params("arbitrary", "arbitrary"),
        name="register",
    )(first, group_ids, shifts, recording)


def filter_kernel(part, taps_ref, x_ref, *refs):
    matrix, rows = refs[-2:]
    out_ref, one, other = refs[-5:-2]
    frames, _, cells, width = x_ref.shape
    planes, tile = out_ref.shape[0], 16
    taps = taps_ref.shape[0]
    reach = (taps - 1) // 2
    t = lax.broadcasted_iota(jnp.int32, (frames, frames), 0)
    u = lax.broadcasted_iota(jnp.int32, (frames, frames), 1)
    distance = u - t + reach
    band = jnp.zeros((frames, frames), jnp.float32)
    for k in range(taps):
        band = jnp.where(distance == k, taps_ref[k], band)
    matrix[...] = (band / jnp.sum(band, axis=1, keepdims=True)).astype(matrix.dtype)

    @pl.loop(0, cells // tile)
    def _(step):
        at = pl.multiple_of(step * tile, tile)
        rows[:frames, :tile] = x_ref[:, part, pl.ds(at, tile)].astype(jnp.float32)
        flat = rows.reshape((frames + 1) * PITCH, width)
        weights = matrix[...]
        for cell in range(tile):
            if cell % 2 == 0:
                two = [flat[pl.ds(cell + k, frames, stride=PITCH), :] for k in range(2)]
                wide = jnp.concatenate([values.astype(jnp.bfloat16) for values in two], axis=1)
                wide = jnp.dot(weights, wide, preferred_element_type=jnp.float32)
            side = cell % 2
            detrended = two[side] - wide[:, side * width : (side + 1) * width]
            average = jnp.sum(detrended, axis=0, keepdims=True) * (1.0 / frames)
            centred = detrended - average
            power = jnp.sum(centred * centred, axis=0, keepdims=True) * (1.0 / frames)
            plane, row = step * 2 + cell // 8, cell % 8
            normed = (centred * lax.rsqrt(power + EPSILON)).astype(out_ref.dtype)
            out_ref[plane, row] = normed
            if part == 0 and HALF - RADIUS <= row < HALF:
                one[plane, row - (HALF - RADIUS)] = normed
            if part == 0 and HALF <= row < HALF + RADIUS:
                other[plane, row - HALF] = normed

    if part == 1:
        ends = refs[0]
        for k in range(RADIUS):
            for slab, plane in ((one, planes - RADIUS + k), (other, k)):
                slab[k, :8] = ends[plane]
                slab[k, 8:] = out_ref[plane]


def filter_cells(registered, fir_taps, part, *before):
    frames, _, cells, width = registered.shape
    planes = cells // 8

    def shape(*size):
        return jax.ShapeDtypeStruct((*size, frames, width), registered.dtype)

    halo = shape(planes, RADIUS) if part == 0 else shape(RADIUS, 16)
    vmem = pl.BlockSpec(memory_space=pltpu.VMEM)
    return pl.pallas_call(
        functools.partial(filter_kernel, part),
        in_specs=[pl.BlockSpec(memory_space=pltpu.SMEM), vmem] + [vmem] * len(before),
        out_specs=[vmem] * 3,
        out_shape=[shape(planes, 8), halo, halo],
        scratch_shapes=[pltpu.VMEM((frames, frames), jnp.bfloat16), pltpu.VMEM((frames + 1, PITCH, width), jnp.float32)],
        cost_estimate=COST,
        compiler_params=params(),
        name="filter",
    )(fir_taps, registered, *before)


def pair_sums(parts, taps):
    total = parts[RADIUS]
    for k in range(RADIUS):
        total = total + taps[k] * (parts[k] + parts[2 * RADIUS - k])
    return total


TAPS_Y = [float(v / KERNEL_Y[RADIUS]) for v in KERNEL_Y]
TAPS_Z = [float(v / KERNEL_Z[RADIUS]) for v in KERNEL_Z]
SCALE = float(KERNEL_Z[RADIUS]) * float(KERNEL_Y[RADIUS])
WINDOW = 2 * RADIUS + 1


def smooth_z(rows, target):
    planes, frames = target.shape[0], target.shape[1]
    for start in range(0, frames, 16):
        parts = [ref[z, row, start : start + 16].astype(jnp.float32) for ref, z, row in rows]
        for z in range(planes):
            target[z, start : start + 16] = pair_sums(parts[z : z + WINDOW], TAPS_Z)


def stack(low, own, high, planes, low_row, own_row, high_row):
    rows = [(low, k, low_row) for k in range(RADIUS)]
    rows += [(own, z, own_row) for z in range(planes)]
    return rows + [(high, k, high_row) for k in range(RADIUS)]


def band_of(matrix):
    width = matrix.shape[1]
    distance = lax.broadcasted_iota(jnp.int32, (width, width), 1) - lax.broadcasted_iota(
        jnp.int32, (width, width), 0
    )
    band = jnp.zeros((width, width), jnp.float32)
    for k in range(WINDOW):
        band = jnp.where(distance == k - RADIUS, float(KERNEL_X[k]), band)
    matrix[:width] = band.astype(matrix.dtype)
    matrix[width:] = jnp.where(distance == 0, -float(KERNEL_X[RADIUS]), 0.0).astype(matrix.dtype)


def row_of_image(mixed, values_of, matrix, out_ref, y):
    for z in range(mixed.shape[0]):
        values = values_of(z)
        both = jnp.concatenate([mixed[z], values], axis=1)
        neighbor = jnp.dot(both, matrix[...], preferred_element_type=jnp.float32)
        total = jnp.sum(values.astype(jnp.float32) * neighbor, axis=0, keepdims=True)
        out_ref[z, pl.ds(y, 1), :] = total * (SCALE / (values.shape[0] * (1.0 - CENTER)))


def inner_kernel(ends, middle, low, high, out_ref, part_ref, *scratch):
    ring, mixed, matrix = scratch
    planes, tile = out_ref.shape[0], out_ref.shape[1]
    frames = ring.shape[2]
    band_of(matrix)
    for row in range(RADIUS):
        ring[row] = jnp.zeros(ring.shape[1:], ring.dtype)

    def first_ends(y):
        return ends, y + HALF, y + HALF

    def inside(y):
        return middle, y - HALF, y + HALF

    def last_ends(y):
        return ends, y - (tile - HALF), y - (tile - HALF)

    def slot(y):
        return lax.rem(y + RADIUS, ring.shape[0])

    def take(y, where):
        own, row, beside = where(y)
        smooth_z(stack(low, own, high, planes, beside, row, beside), ring.at[slot(y)])

    def give_part(y, at):
        for z in range(planes):
            for start in range(0, frames, 32):
                parts = [ring[slot(y + k - RADIUS), z, start : start + 32] for k in range(WINDOW)]
                part_ref[at, z, start : start + 32] = pair_sums(parts, TAPS_Y)

    def give_two(y, *where):
        for z in range(planes):
            for start in range(0, frames, 32):
                parts = [ring[slot(y + k - RADIUS), z, start : start + 32] for k in range(WINDOW + 1)]
                for n in range(2):
                    total = pair_sums(parts[n : n + WINDOW], TAPS_Y)
                    mixed[n, z, start : start + 32] = total.astype(mixed.dtype)
        for n in range(2):
            own, row, _ = where[n](y + n)
            row_of_image(mixed.at[n], lambda z, own=own, row=row: own[z, row], matrix, out_ref, y + n)

    def run(begin, end, taken, *given):
        @pl.loop(0, (end - begin) // 2)
        def _(i):
            y = begin + 2 * i
            take(y, taken)
            take(y + 1, taken)
            if given:
                give_two(y - RADIUS, *given)

    turn = tile - HALF
    pl.loop(0, RADIUS)(lambda y: take(y, first_ends))

    @pl.loop(RADIUS, 2 * RADIUS)
    def _(y):
        pl.when(y < HALF)(lambda: take(y, first_ends))
        pl.when(y >= HALF)(lambda: take(y, inside))
        give_part(y - RADIUS, y - RADIUS)

    run(2 * RADIUS, 2 * RADIUS + 2, inside, first_ends, inside)
    run(2 * RADIUS + 2, turn, inside, inside, inside)
    run(turn, turn + 2, last_ends, inside, inside)
    run(turn + 2, tile, last_ends, inside, last_ends)

    @pl.loop(tile, tile + RADIUS)
    def _(y):
        ring[slot(y)] = jnp.zeros(ring.shape[1:], ring.dtype)
        give_part(y - RADIUS, y - tile + RADIUS)


def outer_kernel(ends, part, image, *refs):
    sides, (out_ref, halo, mixed, matrix) = refs[:-4], refs[-4:]
    planes, tile = out_ref.shape[0], out_ref.shape[1]
    frames = halo.shape[2]
    band_of(matrix)
    out_ref[...] = image[...]

    def side(low, own, high, first, upper):
        @pl.loop(0, RADIUS)
        def _(k):
            smooth_z(stack(low, own, high, planes, first + k, k, first + k), halo.at[k])

        for n in range(RADIUS):
            y = tile - RADIUS + n if upper else n
            taps = [((tile + k if upper else k - RADIUS) - y + RADIUS, k) for k in range(RADIUS)]
            taps = [(TAPS_Y[at], k) for at, k in taps if 0 <= at < WINDOW]
            for z in range(planes):
                for start in range(0, frames, 32):
                    total = part[n + RADIUS * upper, z, start : start + 32]
                    for tap, k in taps:
                        total = total + tap * halo[k, z, start : start + 32]
                    mixed[z, start : start + 32] = total.astype(mixed.dtype)
            row = y - (tile - HALF) if upper else y + HALF
            row_of_image(mixed, lambda z: ends[z, row], matrix, out_ref, y)

    below, above, low_corners, high_corners = sides
    side(low_corners, below, high_corners, 0, 0)
    side(low_corners, above, high_corners, RADIUS, 1)


def inner(ends, middle, slabs, tile):
    planes, _, frames, width = ends.shape
    vmem = pl.BlockSpec(memory_space=pltpu.VMEM)
    return pl.pallas_call(
        inner_kernel,
        in_specs=[vmem] * 4,
        out_specs=[vmem] * 2,
        out_shape=[
            jax.ShapeDtypeStruct((planes, tile, width), jnp.float32),
            jax.ShapeDtypeStruct((2 * RADIUS, planes, frames, width), jnp.float32),
        ],
        scratch_shapes=[
            pltpu.VMEM((WINDOW + 1, planes, frames, width), jnp.float32),
            pltpu.VMEM((2, planes, frames, width), jnp.bfloat16),
            pltpu.VMEM((2 * width, width), jnp.bfloat16),
        ],
        cost_estimate=COST,
        compiler_params=params(),
        name="inner",
    )(ends, middle, *slabs)


def outer(ends, part, image, below, above, corners):
    planes, _, frames, width = ends.shape
    vmem = pl.BlockSpec(memory_space=pltpu.VMEM)
    return pl.pallas_call(
        outer_kernel,
        in_specs=[vmem] * 7,
        out_specs=vmem,
        out_shape=jax.ShapeDtypeStruct(image.shape, jnp.float32),
        scratch_shapes=[
            pltpu.VMEM((RADIUS, planes, frames, width), jnp.float32),
            pltpu.VMEM((planes, frames, width), jnp.bfloat16),
            pltpu.VMEM((2 * width, width), jnp.bfloat16),
        ],
        cost_estimate=COST,
        compiler_params=params(),
        name="outer",
    )(ends, part, image, below, above, *corners)


def body(recording, group_ids, shifts, fir_taps):
    planes, rows = recording.shape[1], recording.shape[2]
    tiles, slabs = lax.axis_size("frames"), lax.axis_size("gz")
    tile = rows // tiles
    first = (lax.axis_index("frames") * recording.shape[0]).reshape(1)

    slots = [t if t // RUN % 2 == 0 else t // RUN * RUN + RUN - 1 - t % RUN for t in range(tiles)]

    def shift(array, axis, by):
        places = slots if axis == "frames" else list(range(lax.axis_size(axis)))
        return lax.ppermute(array, axis, [(p, places[i + by]) for i, p in enumerate(places) if 0 <= i + by < len(places)])

    sent = register(recording, group_ids, shifts, first, slots)
    arrived = lax.all_to_all(sent, "frames", 0, 0)
    arrived = arrived.reshape(-1, *arrived.shape[2:])
    ends, up, down = filter_cells(arrived, fir_taps, 0)
    below, above = shift(up, "frames", 1), shift(down, "frames", -1)
    middle, to_next, to_last = filter_cells(arrived, fir_taps, 1, ends)
    slabs = [shift(to_next, "gz", 1), shift(to_last, "gz", -1)]
    image, part = inner(ends, middle, slabs, tile)
    corners = []
    for at, by in ((planes - RADIUS, 1), (0, -1)):
        both = jnp.concatenate([below[at : at + RADIUS], above[at : at + RADIUS]], axis=1)
        corners.append(shift(both, "gz", by))
    image = outer(ends, part, image, below, above, corners)
    return lax.ppermute(image, "frames", [(p, t) for t, p in enumerate(slots)])


def solution(mesh):
    placed = (P("frames", "gz", None, None), P(), P(), P())
    return jax.shard_map(
        body, mesh=mesh, in_specs=placed, out_specs=P("gz", "frames", None), check_vma=False
    )
```
